128 devices in a mesh: cp: 8 (over z, x_lo), ep: 16 (over x_hi, y, core).
Axes of the slice: x: 4 (x_hi: 2, x_lo: 2; x = x_hi * 2 + x_lo), y: 4, z: 4, core: 2. Of those that a mesh axis runs over, the one named last changes fastest.
Arguments:
- resid: bfloat16 [16, 1024, 2048], P('ep', 'cp'), may hold values from -6 to 6
- query: bfloat16 [16, 1024, 4096], P('ep', 'cp'), may hold values from -100 to 100
- keys: bfloat16 [16, 1024, 512], P('ep', 'cp'), may hold values from -4.5 to 4.5
- values: bfloat16 [16, 1024, 512], P('ep', 'cp'), may hold values from -6 to 6
- out_proj: bfloat16 [4096, 2048], P('cp'), may hold values from -0.09375 to 0.09375
- norm_gain: float32 [2048], replicated, may hold values from 0.4 to 2.5
- expert_ids: int32 [16, 1024, 8], P('ep', 'cp'), may hold values from 0 to 127, all different within a row; in each aligned block of 128 rows (0 to 127, 128 to 255, ..., all dimensions but the last counted through in order) at most 10 rows name the same one
- route_gates: float32 [16, 1024, 8], P('ep', 'cp'), may hold values from 0.05 to 0.3
- w_gate: bfloat16 [128, 2048, 768], P(('cp', 'ep')), may hold values from -0.125 to 0.125
- w_up: bfloat16 [128, 2048, 768], P(('cp', 'ep')), may hold values from -0.125 to 0.125
- w_down: bfloat16 [128, 768, 2048], P(('cp', 'ep')), may hold values from -0.21875 to 0.21875
- cotangent: bfloat16 [16, 1024, 2048], P('ep', 'cp'), may hold values from -6 to 6
Outputs:
- layer_out: bfloat16 [16, 1024, 2048], P('ep', 'cp')
- grad_hidden: float32 [16, 1024, 2048], P('ep', 'cp')
The draws below stay inside these ranges and needn't reach their ends.
Inputs may be any that keep to these rules, and one draw needn't show every extreme that they name: `expert_ids`: each token names 8 different experts; among the 128 tokens of one device (aligned blocks of 128 consecutive positions of a sequence) no expert is named more than 10 times, a bound that some block reaches.
All inputs are finite; a program needn't handle non-finite values.
Results may differ from the reference program's by a relative error of at most 0.015.
Values may be sent and summed in bfloat16 or wider, within the bound.
A program may use at most 192 MiB of HBM per device.

```python
import math
import jax
import jax.numpy as jnp
import numpy as np
from jax import lax

D = 2048
QHEADS = 32
KVHEADS = 4
HEAD = 128
FF = 768
TOPK = 8
TOK_DEV = 128
EXPERTS = 128
SEQ_LEN = 1024
SEQS = 16
CAP = 10
N_CP = 8
N_EP = 16


def base_keys(key):
    shape = (SEQS, SEQ_LEN, KVHEADS * HEAD)
    normal_part = jnp.clip(jax.random.normal(jax.random.fold_in(key, 101), shape, jnp.float32), -4.5, 4.5)
    blended = normal_part
    position = jnp.arange(SEQ_LEN)[None, :, None]
    marked = position % 97 == 48
    return jnp.where(marked, blended, blended)


def draw_keys(key, part):
    result = base_keys(key)
    return result.astype(jnp.bfloat16)


def draw_query(key, part):
    shape = (SEQS, SEQ_LEN, QHEADS * HEAD)
    key = jax.random.fold_in(key, 7)
    result = jnp.clip(jax.random.normal(jax.random.fold_in(key, 1), shape, jnp.float32), -6.0, 6.0)
    return result.astype(jnp.bfloat16)


def levels(key, extent, cuts, least, largest):
    loudness = 1.0
    for dim, parts in cuts:
        steps = jax.random.uniform(jax.random.fold_in(jax.random.fold_in(key, 6), dim), (parts,), jnp.float32, least / len(cuts), largest / len(cuts))
        loudness = loudness * jnp.repeat(jnp.exp(steps), extent[dim] // parts).reshape((-1,) + (1,) * (len(extent) - 1 - dim))
    return loudness


def shared_out(rng, own, number, rows, number_of, top, limit, lean):
    sequence = jax.random.permutation(rng, number_of)
    crowded, ordinary = shares(number_of, rows * top, limit, lean, True), shares(number_of, rows * top, limit, lean, False)
    places = jnp.arange(number_of)

    def named(tallies, rotation):
        used = int((tallies > 0).sum())
        fixed = max(1, used // 4)
        passed = fixed + (places - fixed + rotation * (used - fixed)) % max(1, number_of - fixed)
        return jnp.zeros((number_of,), jnp.int32).at[sequence[jnp.where(places < fixed, places, passed)]].set(jnp.asarray(tallies, jnp.int32))

    tallies = jnp.where(number % 4 == 0, named(crowded, number // 4), named(ordinary, number - number // 4 - 1))
    mixed = jax.random.permutation(jax.random.fold_in(own, 3), number_of)
    donor, taker = mixed[0:number_of // 2 * 2:2], mixed[1:number_of // 2 * 2:2]
    slack = jnp.minimum(tallies[donor] - 1, limit - tallies[taker]) // 2
    slack = jnp.where((donor == sequence[0]) | (taker == sequence[0]) | (tallies[taker] == 0), 0, jnp.maximum(slack, 0))
    passed = jax.random.randint(jax.random.fold_in(own, 4), (number_of // 2,), 0, 1 << 20) % (slack + 1)
    tallies = tallies.at[donor].add(-passed).at[taker].add(passed)
    labels = jnp.searchsorted(jnp.cumsum(tallies), jnp.arange(rows * top), side="right").astype(jnp.int32)
    listing = labels.reshape(top, rows).T
    listing = listing[jax.random.permutation(jax.random.fold_in(own, 1), rows)]
    rotation = jax.random.randint(jax.random.fold_in(own, 2), (rows, 1), 0, top)
    return jnp.take_along_axis(listing, (jnp.arange(top)[None, :] + rotation) % top, axis=1)


def shares(amount, total, most, lean, full):
    loads = [(1 << 20) // math.isqrt(grade ** lean) + 1 for grade in range(1, amount + 1)]
    largest = most if full else min(most, max(-(-total // amount), total * loads[0] // sum(loads)))
    least = 1 if total - largest >= amount - 1 else 0
    given, spare = [largest] + [least] * (amount - 1), total - largest - least * (amount - 1)
    while spare > 0:
        free = [i for i in range(1, amount) if given[i] < largest] or [i for i in range(1, amount) if given[i] < most]
        pool, budget = sum([loads[i] for i in free]), spare
        for i in free:
            more = min(most - given[i], max(1, budget * loads[i] // pool), spare)
            given[i] = given[i] + more
            spare = spare - more
    return np.array(given)


def centred(stream_key, dims, deviation, bound, cuts=(), kind=jnp.bfloat16):
    values = deviation * jax.random.normal(stream_key, dims, jnp.float32)
    if cuts:
        values = values * levels(stream_key, dims, cuts, -0.22, 0.18)
    return jnp.clip(values, -bound, bound).astype(kind)


def setup_inputs(seed: int = 0) -> dict:
    seeds = jax.random.split(jax.random.key(seed), 13)
    resid = centred(seeds[0], (SEQS, SEQ_LEN, D), 1.0, 6.0, ((0, 16), (1, 8)))
    query = draw_query(jax.random.fold_in(seeds[12], 71), 0)
    keys = draw_keys(jax.random.fold_in(seeds[12], 71), 0)
    values = centred(seeds[3], (SEQS, SEQ_LEN, KVHEADS * HEAD), 1.0, 6.0, ((0, 16), (1, 8)))
    out_proj = centred(seeds[4], (QHEADS * HEAD, D), (QHEADS * HEAD) ** -0.5, 0.09375, ((0, 8),))
    norm_gain = jnp.clip(jnp.exp(jax.random.uniform(seeds[5], (D,), jnp.float32, math.log(0.4), math.log(2.5))), 0.4, 2.5)
    expert_ids_keys = jax.random.split(jax.random.fold_in(seeds[6], 1), SEQS * SEQ_LEN // TOK_DEV)
    expert_ids_turns = jax.random.permutation(jax.random.fold_in(seeds[6], 3), SEQS * SEQ_LEN // TOK_DEV)
    expert_ids = jax.vmap(lambda own, number: shared_out(jax.random.fold_in(seeds[6], 2), own, number, TOK_DEV, EXPERTS, TOPK, CAP, 2))(expert_ids_keys, expert_ids_turns).reshape((SEQS, SEQ_LEN, TOPK))
    route_gates = jnp.clip(0.05 + 0.25 * jax.random.uniform(seeds[7], (SEQS, SEQ_LEN, TOPK), jnp.float32) ** levels(seeds[7], (SEQS, SEQ_LEN, TOPK), ((0, 16), (1, 8)), -0.2, 0.2), 0.05, 0.3)
    w_gate = centred(seeds[8], (EXPERTS, D, FF), D ** -0.5, 0.125, ((0, 128),))
    w_up = centred(seeds[9], (EXPERTS, D, FF), D ** -0.5, 0.125, ((0, 128),))
    w_down = centred(seeds[10], (EXPERTS, FF, D), FF ** -0.5, 0.21875, ((0, 128),))
    cotangent = centred(seeds[11], (SEQS, SEQ_LEN, D), 1.0, 6.0, ((0, 16), (1, 8)))
    return {"resid": resid, "query": query, "keys": keys, "values": values, "out_proj": out_proj, "norm_gain": norm_gain, "expert_ids": expert_ids, "route_gates": route_gates, "w_gate": w_gate, "w_up": w_up, "w_down": w_down, "cotangent": cotangent}


EPSILON = 1e-06

def norm_rows(hidden_rows, gain):
    mean_square = lax.optimization_barrier(jnp.mean(hidden_rows * hidden_rows, axis=-1, keepdims=True))
    return hidden_rows * lax.rsqrt(mean_square + EPSILON) * gain

def silu_parts(gate_pre):
    sigmoid_value = jax.nn.sigmoid(gate_pre)
    return (gate_pre * sigmoid_value, sigmoid_value * (1.0 + gate_pre * (1.0 - sigmoid_value)))

def attend_sequence(query_seq, keys_seq, values_seq):
    length = query_seq.shape[0]
    per_group = QHEADS // KVHEADS
    query_heads = query_seq.reshape(length, QHEADS, HEAD).astype(jnp.float32)
    key_heads = jnp.repeat(keys_seq.reshape(length, KVHEADS, HEAD), per_group, axis=1).astype(jnp.float32)
    value_heads = jnp.repeat(values_seq.reshape(length, KVHEADS, HEAD), per_group, axis=1).astype(jnp.float32)
    scores = jnp.einsum('qhd,khd->hqk', query_heads, key_heads) * HEAD ** (-0.5)
    causal = jnp.arange(length)[:, None] >= jnp.arange(length)[None, :]
    scores = jnp.where(causal[None], scores, -jnp.inf)
    highest = lax.optimization_barrier(jnp.max(scores, axis=-1, keepdims=True))
    weights = jnp.exp(scores - highest)
    probs = (weights / lax.optimization_barrier(jnp.sum(weights, axis=-1, keepdims=True))).astype(jnp.bfloat16)
    probs = lax.optimization_barrier(probs)
    attended = jnp.einsum('hqk,khd->qhd', probs.astype(jnp.float32), value_heads)
    return attended.reshape(length, QHEADS * HEAD).astype(jnp.bfloat16)

def reference(resid, query, keys, values, out_proj, norm_gain, expert_ids, route_gates, w_gate, w_up, w_down, cotangent):
    device_count = N_CP * N_EP
    total_rows = TOK_DEV * TOPK

    def by_device(array):
        split = array.reshape((N_EP, N_CP, TOK_DEV) + array.shape[2:])
        order = (1, 0) + tuple(range(2, split.ndim))
        return split.transpose(order).reshape((device_count * TOK_DEV,) + array.shape[2:])

    def from_device(array):
        split = array.reshape((N_CP, N_EP, TOK_DEV) + array.shape[1:])
        order = (1, 0) + tuple(range(2, split.ndim))
        return split.transpose(order).reshape((SEQS, SEQ_LEN) + array.shape[1:])
    attn_all = lax.map(lambda packed: attend_sequence(packed[0], packed[1], packed[2]), (query, keys, values))
    attn_proj = jnp.dot(attn_all.reshape(SEQS * SEQ_LEN, QHEADS * HEAD), out_proj, preferred_element_type=jnp.float32)
    hidden = resid.astype(jnp.float32) + attn_proj.reshape(SEQS, SEQ_LEN, D)
    hidden_dev = by_device(hidden)
    normed_full, pullback = jax.vjp(lambda hidden_rows: norm_rows(hidden_rows, norm_gain), hidden_dev)
    normed = normed_full.astype(jnp.bfloat16)
    ids_dev = by_device(expert_ids).reshape(device_count, total_rows)
    gates_flat = by_device(route_gates).reshape(device_count * total_rows)
    cot_dev = by_device(cotangent)
    onehot = (ids_dev[:, :, None] == jnp.arange(EXPERTS, dtype=jnp.int32)[None, None, :]).astype(jnp.int32)
    ranks = lax.optimization_barrier(jnp.sum(jnp.cumsum(onehot, axis=1) * onehot, axis=2)) - 1
    source = jnp.arange(device_count, dtype=jnp.int32)[:, None] * jnp.ones((1, total_rows), jnp.int32)
    global_row = source * total_rows + jnp.arange(total_rows, dtype=jnp.int32)[None, :]
    table = jnp.full((EXPERTS, device_count * CAP), device_count * total_rows, jnp.int32)
    table = table.at[ids_dev, source * CAP + ranks].set(global_row)
    normed_pad = jnp.concatenate([normed, jnp.zeros((1, D), jnp.bfloat16)], axis=0)
    cot_pad = jnp.concatenate([cot_dev, jnp.zeros((1, D), jnp.bfloat16)], axis=0)
    gates_pad = jnp.concatenate([gates_flat, jnp.zeros((1,), jnp.float32)], axis=0)

    def one_expert(carry, packet):
        moe_sum, normed_grad = carry
        slot_rows, gate_weight, up_weight, down_weight = packet
        token = slot_rows // TOPK
        inputs = normed_pad[token]
        weight = gates_pad[slot_rows]
        gate_pre = jnp.dot(inputs, gate_weight, preferred_element_type=jnp.float32)
        up_pre = jnp.dot(inputs, up_weight, preferred_element_type=jnp.float32)
        silu_value, silu_slope = silu_parts(gate_pre)
        inner = (silu_value * up_pre).astype(jnp.bfloat16)
        expert_out = jnp.dot(inner, down_weight, preferred_element_type=jnp.float32).astype(jnp.bfloat16)
        moe_sum = moe_sum.at[token].add(weight[:, None] * expert_out.astype(jnp.float32), mode='drop')
        grad_rows = (weight[:, None] * cot_pad[token].astype(jnp.float32)).astype(jnp.bfloat16)
        grad_inner = jnp.dot(grad_rows, down_weight.T, preferred_element_type=jnp.float32)
        grad_gate = (grad_inner * up_pre * silu_slope).astype(jnp.bfloat16)
        grad_up = (grad_inner * silu_value).astype(jnp.bfloat16)
        grad_input = jnp.dot(grad_gate, gate_weight.T, preferred_element_type=jnp.float32)
        grad_input = (grad_input + jnp.dot(grad_up, up_weight.T, preferred_element_type=jnp.float32)).astype(jnp.bfloat16)
        normed_grad = normed_grad.at[token].add(grad_input.astype(jnp.float32), mode='drop')
        return ((moe_sum, normed_grad), None)
    start = jnp.zeros((device_count * TOK_DEV, D), jnp.float32)
    (moe_sum, normed_grad), unused = lax.scan(one_expert, (start, start), (table, w_gate, w_up, w_down))
    layer_out = (hidden_dev + moe_sum).astype(jnp.bfloat16)
    grad_hidden = cot_dev.astype(jnp.float32) + pullback(normed_grad)[0]
    return (from_device(layer_out), from_device(grad_hidden))
```

```python
import functools
import jax
import jax.numpy as jnp
from jax import lax
from jax.experimental import pallas as pl
from jax.experimental.pallas import tpu as pltpu
from jax.sharding import PartitionSpec as P

MESH = pl.DeviceIdType.MESH
QHEADS = 32
KVHEADS = 4
HEAD = 128
EPSILON = 1e-06
D = 2048
CAP = 10
BLK = 80
COLS = ((0, 640), (640, 640), (1280, 768))
ROLES = ((2, 0, 1), (0, 1, 2), (1, 2, 0))
F32 = jnp.float32
BF16 = jnp.bfloat16


def coords():
    cp = lax.axis_index("cp")
    ep = lax.axis_index("ep")
    x = lax.div(ep, 8) * 2 + lax.rem(cp, 2)
    y = lax.rem(lax.div(ep, 2), 4)
    z = lax.div(cp, 2)
    return (x, y, z), lax.rem(ep, 2)


def place(pos, core):
    x, y, z = pos
    return (z * 2 + lax.rem(x, 2), lax.div(x, 2) * 8 + y * 2 + core)


def turn(v, d):
    return lax.rem(v + d, 4)


def moved(pos, axis, d):
    return tuple(turn(p, d) if i == axis else p for i, p in enumerate(pos))


class Net:
    def __init__(self, send, recv):
        self.pos, self.core = coords()
        self.send, self.recv = send, recv
        self.count = 0
        self.open = []

    def peer(self, axis, d):
        return place(moved(self.pos, axis, d), self.core)

    def mate(self):
        return place(self.pos, 1 - self.core)

    def copy(self, src, dst, target):
        n = self.count
        self.count += 1
        made = pltpu.make_async_remote_copy(
            src_ref=src, dst_ref=dst, send_sem=self.send.at[n], recv_sem=self.recv.at[n],
            device_id=target, device_id_type=MESH)
        self.open.append(made)
        return made

    def barrier(self):
        bar = pltpu.get_barrier_semaphore()
        targets = [self.peer(a, d) for a in range(3) for d in (1, 2, 3)] + [self.mate()]
        for t in targets:
            pl.semaphore_signal(bar, inc=1, device_id=t, device_id_type=MESH)
        pl.semaphore_wait(bar, len(targets))

    def finish(self):
        for made in self.open:
            made.wait_send()


def swap_matrix():
    r = lax.broadcasted_iota(jnp.int32, (320, 320), 0)
    c = lax.broadcasted_iota(jnp.int32, (320, 320), 1)
    b, rest = lax.div(r, 80), lax.rem(r, 80)
    a, w = lax.div(rest, 20), lax.rem(rest, 20)
    return (c == a * 80 + b * 20 + w).astype(F32).astype(BF16)


def ranks_to(ids_ref, gates_ref, out_ref, t):
    a1, a2, a3 = ROLES[t]
    q = lax.broadcasted_iota(jnp.int32, (128, 128), 0)
    digit = {a1: lax.div(q, 32), a2: lax.rem(lax.div(q, 4), 4), a3: lax.rem(q, 4)}
    core = lax.rem(lax.div(q, 16), 2)
    e0, e1 = place((digit[0], digit[1], digit[2]), core)
    expert = e0 * 16 + e1
    named = jnp.zeros((128, 128), F32)
    gate = jnp.zeros((128, 128), F32)
    for j in range(8):
        hit = ids_ref[j:j + 1, :] == expert
        named = named + jnp.where(hit, 1.0, 0.0)
        gate = gate + jnp.where(hit, gates_ref[j:j + 1, :], 0.0)
    lo = lax.broadcasted_iota(jnp.int32, (128, 128), 0)
    hi = lax.broadcasted_iota(jnp.int32, (128, 128), 1)
    upto = (lo <= hi).astype(F32).astype(BF16)
    seen = jnp.dot(named.astype(BF16), upto, preferred_element_type=F32)
    rank = jnp.where(named > 0.5, seen - 1.0, -1000.0)
    out_ref[:, :, 0] = rank.reshape(4, 2, 16, 128)
    out_ref[:, :, 1] = gate.reshape(4, 2, 16, 128)


def build_pick(ranks, core, pick_ref, gate_ref=None):
    rows = lax.broadcasted_iota(jnp.int32, (BLK, 128), 0).astype(F32)

    def step(e, carry):
        at = pl.multiple_of(e * BLK, 16)
        total = jnp.zeros((BLK, 128), F32)
        for s in range(8):
            rank = ranks[s // 2, s % 2, core, 0, pl.ds(e, 1), :]
            hit = rank + float(CAP * s) == rows
            pick_ref[pl.ds(at, BLK), s * 128:(s + 1) * 128] = jnp.where(hit, 1.0, 0.0).astype(BF16)
            if gate_ref is not None:
                gate = ranks[s // 2, s % 2, core, 1, pl.ds(e, 1), :]
                total = total + jnp.where(hit, gate, 0.0)
        if gate_ref is not None:
            gate_ref[pl.ds(at, BLK), :] = jnp.sum(total, axis=1, keepdims=True)
        return carry
    lax.fori_loop(0, 16, step, 0)


def dispatch_kernel(scaled, x_ref, ids_ref, gates_ref, out_ref, ranks_out, *scratch):
    (ag0, ag1, ag2, sel0, sel1, sel2, mid0, mid1, mid2, end0, end1, end2,
     own_ranks, pick, gate, send, recv) = scratch
    ags, sels, mids, ends = (ag0, ag1, ag2), (sel0, sel1, sel2), (mid0, mid1, mid2), (end0, end1, end2)
    net = Net(send, recv)
    pos, core = net.pos, net.core
    net.barrier()
    gathers, own, rank_sends, mate_ranks = [], [], [], []
    for t in range(3):
        a1 = ROLES[t][0]
        c0, w = COLS[t]
        src = x_ref.at[:, c0:c0 + w]
        slot = pos[a1] * 2 + core
        cps = [net.copy(src, ags[t].at[slot], net.peer(a1, d)) for d in (1, 2, 3)]
        mate = net.copy(src, ags[t].at[slot], net.mate())
        for cp in cps + [mate]:
            cp.start()
        gathers.append(cps)
        own.append(mate)
    for t in range(3):
        a1 = ROLES[t][0]
        c0, w = COLS[t]
        ags[t][pos[a1] * 2 + core] = x_ref[:, c0:c0 + w]
        ranks_to(ids_ref, gates_ref, own_ranks.at[t], t)
        cps = [net.copy(own_ranks.at[t, turn(pos[a1], d)], ranks_out.at[t, pos[a1], core], net.peer(a1, d)) for d in (1, 2, 3)]
        for cp in cps:
            cp.start()
        ranks_out[t, pos[a1], core] = own_ranks[t, pos[a1]]
        mate = net.copy(own_ranks.at[t, pos[a1], 1 - core], ranks_out.at[t, pos[a1], core, 1 - core], net.mate())
        mate.start()
        rank_sends.append(cps)
        mate_ranks.append([mate])
    forwards = []
    for t in range(3):
        a1 = ROLES[t][0]
        fw = []
        for i, d in enumerate((1, 2, 3)):
            rank_sends[t][i].wait_recv()
            a = turn(pos[a1], 4 - d)
            cp = net.copy(ranks_out.at[t, a, core, 1 - core], ranks_out.at[t, a, core, 1 - core], net.mate())
            cp.start()
            mate_ranks[t].append(cp)
    for t in range(3):
        a1 = ROLES[t][0]
        fw = []
        for i, d in enumerate((1, 2, 3)):
            gathers[t][i].wait_recv()
            s = turn(pos[a1], 4 - d) * 2 + core
            cp = net.copy(ags[t].at[s], ags[t].at[s], net.mate())
            cp.start()
            fw.append(cp)
        forwards.append(fw)
    firsts = []
    for t in range(3):
        a1, a2, a3 = ROLES[t]
        w = COLS[t][1]
        for cp in mate_ranks[t]:
            cp.wait_recv()
        build_pick(ranks_out.at[t], core, pick, gate if scaled else None)
        own[t].wait_recv()
        for cp in forwards[t]:
            cp.wait_recv()
        base = net.count
        cps = [net.copy(sels[t].at[d - 1], mids[t].at[pos[a2]], net.peer(a2, d)) for d in (1, 2, 3)]

        def chosen(b):
            at = pl.multiple_of(b * 320, 16)
            rows = jnp.dot(pick[pl.ds(at, 320), :], ags[t][...].reshape(1024, w), preferred_element_type=F32)
            if scaled:
                rows = rows * gate[pl.ds(at, 320), :]
            return rows.astype(BF16).reshape(4, BLK, w)
        for d in (1, 2, 3):
            sels[t][d - 1] = chosen(turn(pos[a2], d))
            cps[d - 1].start()
        mids[t][pos[a2]] = chosen(pos[a2])
        firsts.append(cps)
    seconds = []
    for t in range(3):
        a1, a2, a3 = ROLES[t]
        sec = []
        for i in range(4):
            a = turn(pos[a2], 4 - i)
            if i:
                firsts[t][i - 1].wait_recv()
            for d in (1, 2, 3):
                cp = net.copy(mids[t].at[a, turn(pos[a3], d)], ends[t].at[pos[a3], a], net.peer(a3, d))
                cp.start()
                sec.append(cp)
            ends[t][pos[a3], a] = mids[t][a, pos[a3]]
        seconds.append(sec)
    swap = swap_matrix()
    for t in range(3):
        c0, w = COLS[t]
        for cp in seconds[t]:
            cp.wait_recv()
        for g in range(4):
            if t == 0:
                out_ref[g * 320:(g + 1) * 320, c0:c0 + w] = ends[t][g].reshape(320, w)
            elif t == 1:
                got = jnp.dot(swap, ends[t][:, g].reshape(320, w), preferred_element_type=F32).astype(BF16)
                out_ref[g * 320:(g + 1) * 320, c0:c0 + w] = got
            else:
                got = jnp.dot(swap, ends[t][g].reshape(320, w), preferred_element_type=F32).astype(BF16)
                for y in range(4):
                    out_ref[y * 320 + g * BLK:y * 320 + (g + 1) * BLK, c0:c0 + w] = got[y * BLK:(y + 1) * BLK]
    net.finish()


def vm(*shape, dtype=BF16):
    return pltpu.VMEM(shape, dtype)


def dispatch(x, ids_t, gates_t, scaled, cid):
    v = pl.BlockSpec(memory_space=pltpu.VMEM)
    ws = [w for _, w in COLS]
    return pl.pallas_call(
        functools.partial(dispatch_kernel, scaled),
        out_shape=(jax.ShapeDtypeStruct((1280, D), BF16), jax.ShapeDtypeStruct((3, 4, 2, 2, 2, 16, 128), F32)),
        in_specs=[v] * 3, out_specs=(v, v),
        scratch_shapes=[vm(8, 128, w) for w in ws] + [vm(3, 4, BLK, w) for w in ws] + [vm(4, 4, BLK, w) for w in ws]
        + [vm(4, 4, BLK, w) for w in ws] + [vm(3, 4, 2, 2, 16, 128, dtype=F32), vm(1280, 1024), vm(1280, 1, dtype=F32),
                                            pltpu.SemaphoreType.DMA((120,)), pltpu.SemaphoreType.DMA((120,))],
        compiler_params=pltpu.CompilerParams(collective_id=cid, has_side_effects=True, vmem_limit_bytes=60 * 2**20),
    )(x, ids_t, gates_t)


def return_kernel(eo_ref, gi_ref, ranks, moe_ref, grad_ref, *scratch):
    (m0, m1, m2, o0, o1, o2, n0, n1, n2, part0, part1, part2, core0, core1, core2, rs0, rs1, rs2, pick, gate, send, recv, local) = scratch
    outs, mids, news = (o0, o1, o2), (m0, m1, m2), (n0, n1, n2)
    parts, cores, rss = (part0, part1, part2), (core0, core1, core2), (rs0, rs1, rs2)
    net = Net(send, recv)
    pos, core = net.pos, net.core
    net.barrier()
    swap = swap_matrix()
    srcs = (eo_ref, gi_ref)
    phase1 = {}
    for k in range(2):
        for t in range(3):
            a1, a2, a3 = ROLES[t]
            c0, w = COLS[t]
            o = outs[t].at[k]
            for g in range(4):
                if t == 0:
                    o[g] = srcs[k][g * 320:(g + 1) * 320, c0:c0 + w].reshape(4, BLK, w)
                elif t == 1:
                    got = jnp.dot(swap, srcs[k][g * 320:(g + 1) * 320, c0:c0 + w], preferred_element_type=F32).astype(BF16)
                    o[:, g] = got.reshape(4, BLK, w)
                else:
                    rows = jnp.concatenate([srcs[k][y * 320 + g * BLK:y * 320 + (g + 1) * BLK, c0:c0 + w] for y in range(4)], axis=0)
                    o[g] = jnp.dot(swap, rows, preferred_element_type=F32).astype(BF16).reshape(4, BLK, w)
            cps = []
            for d in (1, 2, 3):
                cp = net.copy(o.at[turn(pos[a3], d)], mids[t].at[k, pos[a3]], net.peer(a3, d))
                cp.start()
                cps.append(cp)
            phase1[k, t] = cps
    phase2, kept = {}, {}
    for k in range(2):
        for t in range(3):
            a1, a2, a3 = ROLES[t]
            cps = []
            kept[k, t] = []
            for i in range(4):
                a = turn(pos[a3], 4 - i)
                if i:
                    phase1[k, t][i - 1].wait_recv()
                    here = mids[t].at[k, a]
                else:
                    here = outs[t].at[k, a]
                for d in (1, 2, 3):
                    cp = net.copy(here.at[turn(pos[a2], d)], news[t].at[k, pos[a2], a], net.peer(a2, d))
                    cp.start()
                    cps.append(cp)
                keep = pltpu.make_async_copy(here.at[pos[a2]], news[t].at[k, pos[a2], a], local.at[k * 12 + t * 4 + i])
                keep.start()
                kept[k, t].append(keep)
            phase2[k, t] = cps
    phase3 = {}
    for k in range(2):
        for t in range(3):
            a1, a2, a3 = ROLES[t]
            c0, w = COLS[t]
            build_pick(ranks.at[t], core, pick, gate)
            for cp in phase2[k, t]:
                cp.wait_recv()
            for keep in kept[k, t]:
                keep.wait()
            rows = news[t][k].reshape(1280, w)
            if k == 0:
                rows = (rows.astype(F32) * gate[...]).astype(BF16)
            total = lax.dot_general(pick[...], rows, (((0,), (0,)), ((), ())), preferred_element_type=F32)
            parts[t][k] = total.astype(BF16).reshape(4, 2, 128, w)
            cp = net.copy(parts[t].at[k, :, 1 - core], cores[t].at[k], net.mate())
            cp.start()
            phase3[k, t] = cp
    phase4 = {}
    for k in range(2):
        for t in range(3):
            a1 = ROLES[t][0]
            phase3[k, t].wait_recv()
            cores[t][k] = (cores[t][k].astype(F32) + parts[t][k, :, core].astype(F32)).astype(BF16)
            cps = []
            for d in (1, 2, 3):
                cp = net.copy(cores[t].at[k, turn(pos[a1], d)], rss[t].at[k, d - 1], net.peer(a1, d))
                cp.start()
                cps.append(cp)
            phase4[k, t] = cps
    dst = (moe_ref, grad_ref)
    for k in range(2):
        for t in range(3):
            a1 = ROLES[t][0]
            c0, w = COLS[t]
            total = cores[t][k, pos[a1]].astype(F32)
            for i, cp in enumerate(phase4[k, t]):
                cp.wait_recv()
                total = total + rss[t][k, i].astype(F32)
            dst[k][:, c0:c0 + w] = total
    net.finish()


def give_back(eo, gi, ranks, cid):
    v = pl.BlockSpec(memory_space=pltpu.VMEM)
    ws = [w for _, w in COLS]
    shape = jax.ShapeDtypeStruct((128, D), F32)
    return pl.pallas_call(
        return_kernel,
        out_shape=(shape, shape) + tuple(jax.ShapeDtypeStruct((2, 4, 4, BLK, w), BF16) for w in ws),
        in_specs=[v] * 3, out_specs=(v, v) + (pl.BlockSpec(memory_space=pl.ANY),) * 3,
        scratch_shapes=[vm(2, 4, 4, BLK, w) for w in ws] + [vm(2, 4, 4, BLK, w) for w in ws]
        + [vm(2, 4, 2, 128, w) for w in ws] + [vm(2, 4, 128, w) for w in ws] + [vm(2, 3, 128, w) for w in ws]
        + [vm(1280, 1024), vm(1280, 1, dtype=F32), pltpu.SemaphoreType.DMA((200,)), pltpu.SemaphoreType.DMA((200,)),
           pltpu.SemaphoreType.DMA((24,))],
        compiler_params=pltpu.CompilerParams(collective_id=cid, has_side_effects=True, vmem_limit_bytes=63 * 2**20),
    )(eo, gi, ranks)[:2]


def norm_rows(hidden_rows, gain):
    mean_square = jnp.mean(hidden_rows * hidden_rows, axis=-1, keepdims=True)
    return hidden_rows * lax.rsqrt(mean_square + EPSILON) * gain


def silu_parts(gate_pre):
    sigmoid_value = jax.nn.sigmoid(gate_pre)
    return (gate_pre * sigmoid_value, sigmoid_value * (1.0 + gate_pre * (1.0 - sigmoid_value)))


def on_device(
    resid,
    query,
    keys,
    values,
    out_proj,
    norm_gain,
    expert_ids,
    route_gates,
    w_gate,
    w_up,
    w_down,
    cotangent,
):
    cp_count = lax.axis_size("cp")
    ep_count = lax.axis_size("ep")
    tok_rows = resid.shape[1]
    model_width = resid.shape[2]
    seq_rows = tok_rows * cp_count
    kv_repeat = max(cp_count // KVHEADS, 1)

    def widen(source):
        split_heads = source[0].reshape(tok_rows, KVHEADS, HEAD)
        return jnp.repeat(split_heads, kv_repeat, axis=1).reshape(
            tok_rows, KVHEADS * kv_repeat * HEAD
        )

    head_query, head_keys, head_values = (
        lax.all_to_all(query[0], "cp", split_axis=1, concat_axis=0, tiled=True),
        lax.all_to_all(widen(keys), "cp", split_axis=1, concat_axis=0, tiled=True),
        lax.all_to_all(widen(values), "cp", split_axis=1, concat_axis=0, tiled=True),
    )
    local_heads = QHEADS // cp_count
    local_kv = KVHEADS * kv_repeat // cp_count
    per_group = local_heads // local_kv
    grouped_query = head_query.reshape(seq_rows, local_kv, per_group, HEAD)
    grouped_keys = head_keys.reshape(seq_rows, local_kv, HEAD)
    grouped_values = head_values.reshape(seq_rows, local_kv, HEAD)
    scores = jnp.einsum(
        "qagd,kad->agqk", grouped_query, grouped_keys, preferred_element_type=jnp.float32
    ) * HEAD ** (-0.5)
    causal = lax.broadcasted_iota(jnp.int32, (seq_rows, seq_rows), 0) >= lax.broadcasted_iota(
        jnp.int32, (seq_rows, seq_rows), 1
    )
    scores = jnp.where(causal[None, None], scores, -jnp.inf)
    highest = jnp.max(scores, axis=-1, keepdims=True)
    weights = jnp.exp(scores - highest)
    probs = (weights / jnp.sum(weights, axis=-1, keepdims=True)).astype(jnp.bfloat16)
    attended = jnp.einsum(
        "agqk,kad->qagd", probs, grouped_values, preferred_element_type=jnp.float32
    )
    attn_out = attended.reshape(seq_rows, local_heads * HEAD).astype(jnp.bfloat16)
    attn_proj = lax.psum_scatter(
        jnp.dot(attn_out, out_proj, preferred_element_type=jnp.float32).astype(jnp.bfloat16),
        "cp",
        scatter_dimension=0,
        tiled=True,
    ).astype(jnp.float32)
    hidden = resid[0].astype(jnp.float32) + attn_proj
    normed_full, pullback = jax.vjp(lambda hidden_rows: norm_rows(hidden_rows, norm_gain), hidden)
    normed = normed_full.astype(jnp.bfloat16)
    ids_t = expert_ids[0].T
    gates_t = route_gates[0].T
    gate_weight = w_gate[0]
    up_weight = w_up[0]
    down_weight = w_down[0]
    cot_rows = cotangent[0]
    grad_arrived, _ = dispatch(cot_rows, ids_t, gates_t, True, 5)
    arrived, ranks = dispatch(normed, ids_t, gates_t, False, 6)
    gate_pre = jnp.dot(arrived, gate_weight, preferred_element_type=jnp.float32)
    up_pre = jnp.dot(arrived, up_weight, preferred_element_type=jnp.float32)
    silu_value, silu_slope = silu_parts(gate_pre)
    inner = (silu_value * up_pre).astype(jnp.bfloat16)
    expert_out = jnp.dot(inner, down_weight, preferred_element_type=jnp.float32).astype(
        jnp.bfloat16
    )
    contract_last = (((1,), (1,)), ((), ()))
    grad_inner = lax.dot_general(
        grad_arrived, down_weight, contract_last, preferred_element_type=jnp.float32
    )
    grad_gate = (grad_inner * up_pre * silu_slope).astype(jnp.bfloat16)
    grad_up = (grad_inner * silu_value).astype(jnp.bfloat16)
    grad_input = lax.dot_general(
        grad_gate, gate_weight, contract_last, preferred_element_type=jnp.float32
    )
    grad_input = grad_input + lax.dot_general(
        grad_up, up_weight, contract_last, preferred_element_type=jnp.float32
    )
    grad_input = grad_input.astype(jnp.bfloat16)
    moe_sum, normed_grad = give_back(expert_out, grad_input, ranks, 7)
    layer_out = (hidden + moe_sum).astype(jnp.bfloat16)
    grad_hidden = cot_rows.astype(jnp.float32) + pullback(normed_grad)[0]
    return (layer_out[None], grad_hidden[None])


def solution(mesh):
    placed = (
        P("ep", "cp", None),
        P("ep", "cp", None),
        P("ep", "cp", None),
        P("ep", "cp", None),
        P("cp", None),
        P(),
        P("ep", "cp", None),
        P("ep", "cp", None),
        P(("cp", "ep"), None, None),
        P(("cp", "ep"), None, None),
        P(("cp", "ep"), None, None),
        P("ep", "cp", None),
    )
    return jax.shard_map(
        on_device,
        mesh=mesh,
        in_specs=placed,
        out_specs=(P("ep", "cp", None), P("ep", "cp", None)),
        check_vma=False,
    )
```

```python
import functools
import jax
import jax.numpy as jnp
from jax import lax
from jax.experimental import pallas as pl
from jax.experimental.pallas import tpu as pltpu
from jax.sharding import PartitionSpec as P

MESH = pl.DeviceIdType.MESH
D = 2048
EPSILON = 1e-06
HEAD = 128
CAP = 10
BLK = 80
COLS = ((0, 640), (640, 640), (1280, 768))
ROLES = ((2, 0, 1), (0, 1, 2), (1, 2, 0))
F32 = jnp.float32
BF16 = jnp.bfloat16


def coords():
    cp = lax.axis_index("cp")
    ep = lax.axis_index("ep")
    x = lax.div(ep, 8) * 2 + lax.rem(cp, 2)
    y = lax.rem(lax.div(ep, 2), 4)
    z = lax.div(cp, 2)
    return (x, y, z), lax.rem(ep, 2)


def place(pos, core):
    x, y, z = pos
    return (z * 2 + lax.rem(x, 2), lax.div(x, 2) * 8 + y * 2 + core)


def turn(v, d):
    return lax.rem(v + d, 4)


def moved(pos, axis, d):
    return tuple(turn(p, d) if i == axis else p for i, p in enumerate(pos))


class Net:
    def __init__(self, send, recv):
        self.pos, self.core = coords()
        self.send, self.recv = send, recv
        self.count = 0
        self.open = []

    def peer(self, axis, d):
        return place(moved(self.pos, axis, d), self.core)

    def mate(self):
        return place(self.pos, 1 - self.core)

    def copy(self, src, dst, target):
        n = self.count
        self.count += 1
        made = pltpu.make_async_remote_copy(
            src_ref=src, dst_ref=dst, send_sem=self.send.at[n], recv_sem=self.recv.at[n],
            device_id=target, device_id_type=MESH)
        self.open.append(made)
        return made

    def barrier(self, more=()):
        bar = pltpu.get_barrier_semaphore()
        targets = list(more) + [self.peer(a, d) for a in range(3) for d in (1, 2, 3)] + [self.mate()]
        for t in targets:
            pl.semaphore_signal(bar, inc=1, device_id=t, device_id_type=MESH)
        pl.semaphore_wait(bar, len(targets))

    def finish(self):
        for made in self.open:
            made.wait_send()


def swap_matrix():
    r = lax.broadcasted_iota(jnp.int32, (320, 320), 0)
    c = lax.broadcasted_iota(jnp.int32, (320, 320), 1)
    b, rest = lax.div(r, 80), lax.rem(r, 80)
    a, w = lax.div(rest, 20), lax.rem(rest, 20)
    return (c == a * 80 + b * 20 + w).astype(F32).astype(BF16)


def ranks_to(ids_ref, gates_ref, out_ref, t):
    a1, a2, a3 = ROLES[t]
    q = lax.broadcasted_iota(jnp.int32, (128, 128), 0)
    digit = {a1: lax.div(q, 32), a2: lax.rem(lax.div(q, 4), 4), a3: lax.rem(q, 4)}
    core = lax.rem(lax.div(q, 16), 2)
    e0, e1 = place((digit[0], digit[1], digit[2]), core)
    expert = e0 * 16 + e1
    named = jnp.zeros((128, 128), F32)
    gate = jnp.zeros((128, 128), F32)
    for j in range(8):
        hit = ids_ref[j:j + 1, :] == expert
        named = named + jnp.where(hit, 1.0, 0.0)
        gate = gate + jnp.where(hit, gates_ref[j:j + 1, :], 0.0)
    lo = lax.broadcasted_iota(jnp.int32, (128, 128), 0)
    hi = lax.broadcasted_iota(jnp.int32, (128, 128), 1)
    upto = (lo <= hi).astype(F32).astype(BF16)
    seen = jnp.dot(named.astype(BF16), upto, preferred_element_type=F32)
    rank = jnp.where(named > 0.5, seen - 1.0, -1000.0)
    out_ref[:, :, 0] = rank.reshape(4, 2, 16, 128)
    out_ref[:, :, 1] = gate.reshape(4, 2, 16, 128)


def build_pick(ranks, core, pick_ref, gate_ref=None):
    rows = lax.broadcasted_iota(jnp.int32, (BLK, 128), 0).astype(F32)

    def step(e, carry):
        at = pl.multiple_of(e * BLK, 16)
        total = jnp.zeros((BLK, 128), F32)
        for s in range(8):
            rank = ranks[s // 2, s % 2, core, 0, pl.ds(e, 1), :]
            hit = rank + float(CAP * s) == rows
            pick_ref[pl.ds(at, BLK), s * 128:(s + 1) * 128] = jnp.where(hit, 1.0, 0.0).astype(BF16)
            if gate_ref is not None:
                gate = ranks[s // 2, s % 2, core, 1, pl.ds(e, 1), :]
                total = total + jnp.where(hit, gate, 0.0)
        if gate_ref is not None:
            gate_ref[pl.ds(at, BLK), :] = jnp.sum(total, axis=1, keepdims=True)
        return carry
    lax.fori_loop(0, 16, step, 0)


class Dispatch:
    def __init__(self, net, scaled, ags, sels, mids, ends, own_ranks, ranks, pick, gate):
        self.net, self.scaled = net, scaled
        self.ags, self.sels, self.mids, self.ends = ags, sels, mids, ends
        self.own_ranks, self.ranks, self.pick, self.gate = own_ranks, ranks, pick, gate
        self.gathers, self.own, self.rank_sends, self.mate_ranks = [], [], [], []
        self.forwards, self.firsts, self.seconds = [], [], []

    def gather(self, x_ref):
        net, pos, core = self.net, self.net.pos, self.net.core
        for t in range(3):
            a1 = ROLES[t][0]
            c0, w = COLS[t]
            src = x_ref.at[:, c0:c0 + w]
            slot = pos[a1] * 2 + core
            cps = [net.copy(src, self.ags[t].at[slot], net.peer(a1, d)) for d in (1, 2, 3)]
            mate = net.copy(src, self.ags[t].at[slot], net.mate())
            for cp in cps + [mate]:
                cp.start()
            self.gathers.append(cps)
            self.own.append(mate)
        for t in range(3):
            a1 = ROLES[t][0]
            c0, w = COLS[t]
            self.ags[t][pos[a1] * 2 + core] = x_ref[:, c0:c0 + w]

    def send_ranks(self, ids_ref, gates_ref):
        net, pos, core = self.net, self.net.pos, self.net.core
        own_ranks, ranks = self.own_ranks, self.ranks
        for t in range(3):
            a1 = ROLES[t][0]
            ranks_to(ids_ref, gates_ref, own_ranks.at[t], t)
            cps = [net.copy(own_ranks.at[t, turn(pos[a1], d)], ranks.at[t, pos[a1], core], net.peer(a1, d)) for d in (1, 2, 3)]
            for cp in cps:
                cp.start()
            ranks[t, pos[a1], core] = own_ranks[t, pos[a1]]
            mate = net.copy(own_ranks.at[t, pos[a1], 1 - core], ranks.at[t, pos[a1], core, 1 - core], net.mate())
            mate.start()
            self.rank_sends.append(cps)
            self.mate_ranks.append([mate])

    def forward_ranks(self):
        net, pos, core, ranks = self.net, self.net.pos, self.net.core, self.ranks
        for t in range(3):
            a1 = ROLES[t][0]
            for i, d in enumerate((1, 2, 3)):
                self.rank_sends[t][i].wait_recv()
                a = turn(pos[a1], 4 - d)
                cp = net.copy(ranks.at[t, a, core, 1 - core], ranks.at[t, a, core, 1 - core], net.mate())
                cp.start()
                self.mate_ranks[t].append(cp)

    def wait_ranks(self, t):
        for cp in self.mate_ranks[t]:
            cp.wait_recv()

    def forward(self):
        net, pos, core = self.net, self.net.pos, self.net.core
        for t in range(3):
            a1 = ROLES[t][0]
            fw = []
            for i, d in enumerate((1, 2, 3)):
                self.gathers[t][i].wait_recv()
                s = turn(pos[a1], 4 - d) * 2 + core
                cp = net.copy(self.ags[t].at[s], self.ags[t].at[s], net.mate())
                cp.start()
                fw.append(cp)
            self.forwards.append(fw)

    def select(self, t):
        net, pos, core = self.net, self.net.pos, self.net.core
        a1, a2, a3 = ROLES[t]
        w = COLS[t][1]
        build_pick(self.ranks.at[t], core, self.pick, self.gate if self.scaled else None)
        self.own[t].wait_recv()
        for cp in self.forwards[t]:
            cp.wait_recv()
        sel, mid = self.sels[t], self.mids[t]
        cps = [net.copy(sel.at[d - 1], mid.at[pos[a2]], net.peer(a2, d)) for d in (1, 2, 3)]

        def chosen(b):
            at = pl.multiple_of(b * 320, 16)
            rows = jnp.dot(self.pick[pl.ds(at, 320), :], self.ags[t][...].reshape(1024, w), preferred_element_type=F32)
            if self.scaled:
                rows = rows * self.gate[pl.ds(at, 320), :]
            return rows.astype(BF16).reshape(4, BLK, w)
        for d in (1, 2, 3):
            sel[d - 1] = chosen(turn(pos[a2], d))
            cps[d - 1].start()
        mid[pos[a2]] = chosen(pos[a2])
        self.firsts.append(cps)

    def second(self, t):
        net, pos = self.net, self.net.pos
        a1, a2, a3 = ROLES[t]
        mid, end = self.mids[t], self.ends[t]
        sec = []
        for i in range(4):
            a = turn(pos[a2], 4 - i)
            if i:
                self.firsts[t][i - 1].wait_recv()
            for d in (1, 2, 3):
                cp = net.copy(mid.at[a, turn(pos[a3], d)], end.at[pos[a3], a], net.peer(a3, d))
                cp.start()
                sec.append(cp)
            end[pos[a3], a] = mid[a, pos[a3]]
        self.seconds.append(sec)

    def arrive(self, t, out_ref, swap):
        c0, w = COLS[t]
        end = self.ends[t]
        for cp in self.seconds[t]:
            cp.wait_recv()
        for g in range(4):
            if t == 0:
                out_ref[g * 320:(g + 1) * 320, c0:c0 + w] = end[g].reshape(320, w)
            elif t == 1:
                got = jnp.dot(swap, end[:, g].reshape(320, w), preferred_element_type=F32).astype(BF16)
                out_ref[g * 320:(g + 1) * 320, c0:c0 + w] = got
            else:
                got = jnp.dot(swap, end[g].reshape(320, w), preferred_element_type=F32).astype(BF16)
                for y in range(4):
                    out_ref[y * 320 + g * BLK:y * 320 + (g + 1) * BLK, c0:c0 + w] = got[y * BLK:(y + 1) * BLK]


def dispatch_kernel(scaled, x_ref, ids_ref, gates_ref, out_ref, ranks_out, *scratch):
    (ag0, ag1, ag2, sel0, sel1, sel2, mid0, mid1, mid2, end0, end1, end2,
     own_ranks, pick, gate, send, recv) = scratch
    net = Net(send, recv)
    net.barrier()
    work = Dispatch(net, scaled, (ag0, ag1, ag2), (sel0, sel1, sel2), (mid0, mid1, mid2), (end0, end1, end2),
                    own_ranks, ranks_out, pick, gate)
    work.gather(x_ref)
    work.send_ranks(ids_ref, gates_ref)
    work.forward_ranks()
    work.forward()
    for t in range(3):
        work.wait_ranks(t)
        work.select(t)
    for t in range(3):
        work.second(t)
    swap = swap_matrix()
    for t in range(3):
        work.arrive(t, out_ref, swap)
    net.finish()


def front_kernel(q_ref, k_ref, v_ref, w_ref, resid_ref, gain_ref, cot_ref, ids_ref, gates_ref,
                 hidden_ref, normed_ref, out_ref, ranks_out, *scratch):
    (ag0, ag1, ag2, sel0, sel1, sel2, mid0, mid1, mid2, end0, end1, end2,
     own_ranks, pick, gate, qbuf, kbuf, vbuf, wbuf, att, part, rs, send, recv, local) = scratch
    net = Net(send, recv)
    pos, core = net.pos, net.core
    x, y, z = pos
    side = lax.rem(x, 2)
    other = x + 1 - 2 * side
    net.barrier([place((other, y, turn(z, d)), core) for d in (1, 2, 3)])
    work = Dispatch(net, True, (ag0, ag1, ag2), (sel0, sel1, sel2), (mid0, mid1, mid2), (end0, end1, end2),
                    own_ranks, ranks_out, pick, gate)
    block = z * 2 + side

    def heads(ref, group, width):
        return ref.at[:, pl.ds(pl.multiple_of(group * width, width), width)]
    moves = []
    for d in (1, 2, 3):
        g = turn(z, d)
        moves.append(net.copy(heads(q_ref, g, 1024), qbuf.at[z], net.peer(2, d)))
    for d in (1, 2, 3, 0):
        g = turn(z, d)
        for xx in (x, other):
            if d or xx is other:
                for ref, buf in ((k_ref, kbuf), (v_ref, vbuf)):
                    moves.append(net.copy(heads(ref, g, 128), buf.at[block], place((xx, y, g), core)))
    for cp in moves:
        cp.start()
    keeps = [pltpu.make_async_copy(heads(q_ref, z, 1024), qbuf.at[z], local.at[0]),
             pltpu.make_async_copy(heads(k_ref, z, 128), kbuf.at[block], local.at[1]),
             pltpu.make_async_copy(heads(v_ref, z, 128), vbuf.at[block], local.at[2]),
             pltpu.make_async_copy(w_ref, wbuf.at[side], local.at[3])]
    for cp in keeps:
        cp.start()
    work.gather(cot_ref)
    work.send_ranks(ids_ref, gates_ref)
    quarters = []
    for i, d in enumerate((1, 3)):
        at = pl.ds(pl.multiple_of((core * 2 + i) * 128, 128), 128)
        cp = net.copy(w_ref.at[at], wbuf.at[side, at], net.peer(0, d))
        cp.start()
        quarters.append(cp)
    work.forward_ranks()
    work.forward()
    for t in range(3):
        work.wait_ranks(t)
        work.select(t)
    for cp in quarters:
        cp.wait_recv()
    at = pl.ds(pl.multiple_of(core * 256, 256), 256)
    half = net.copy(wbuf.at[1 - side, at], wbuf.at[1 - side, at], net.mate())
    half.start()
    for cp in moves:
        cp.wait_recv()
    for cp in keeps:
        cp.wait()
    sends = []
    for zp in (3, 2, 1, 0):
        span = 256 * (zp + 1)

        def pair(i, carry):
            lanes = pl.multiple_of(i * 256, 256)
            two = qbuf[zp, :, pl.ds(lanes, 256)]
            rows = jnp.concatenate([two[:, :128], two[:, 128:]], axis=0)
            scores = lax.dot_general(rows, kbuf[0:2 * zp + 2].reshape(span, 128), (((1,), (1,)), ((), ())),
                                     preferred_element_type=F32) * HEAD ** (-0.5)
            row = lax.broadcasted_iota(jnp.int32, (256, span), 0)
            col = lax.broadcasted_iota(jnp.int32, (256, span), 1)
            seen = col <= lax.rem(row, 128) + (2 * zp + side) * 128
            scores = jnp.where(seen, scores, -jnp.inf)
            weights = jnp.exp(scores - jnp.max(scores, axis=1, keepdims=True))
            probs = (weights / jnp.sum(weights, axis=1, keepdims=True)).astype(BF16)
            got = jnp.dot(probs, vbuf[0:2 * zp + 2].reshape(span, 128), preferred_element_type=F32).astype(BF16)
            att[zp, :, pl.ds(lanes, 256)] = jnp.concatenate([got[:128], got[128:]], axis=1)
            return carry
        lax.fori_loop(0, 4, pair, 0)
        if zp == 3:
            half.wait_recv()

        def project(i, carry):
            lanes = pl.ds(pl.multiple_of(i * 512, 512), 512)
            total = jnp.dot(att[zp], wbuf[:, :, lanes].reshape(1024, 512), preferred_element_type=F32)
            part[zp, :, lanes] = total.astype(BF16)
            return carry
        lax.fori_loop(0, 4, project, 0)
        far = lax.rem(zp + 4 - z, 4)
        slot = lax.rem(far + 3, 4)
        cp = pltpu.make_async_remote_copy(
            src_ref=part.at[zp], dst_ref=rs.at[slot], send_sem=local.at[4 + zp], recv_sem=local.at[8 + slot],
            device_id=place((x, y, zp), core), device_id_type=MESH)

        @pl.when(zp != z)
        def _():
            cp.start()
        sends.append(cp)
    for t in range(3):
        work.second(t)
    total = resid_ref[...].astype(F32) + part[z].astype(F32)
    for d in (1, 2, 3):
        pltpu.make_async_remote_copy(
            src_ref=part.at[0], dst_ref=rs.at[d - 1], send_sem=local.at[4], recv_sem=local.at[7 + d],
            device_id=net.peer(2, d), device_id_type=MESH).wait_recv()
        total = total + rs[d - 1].astype(F32)
    hidden_ref[...] = total
    scale = lax.rsqrt(jnp.mean(total * total, axis=1, keepdims=True) + EPSILON)
    normed_ref[...] = (total * scale * gain_ref[...]).astype(BF16)
    swap = swap_matrix()
    for t in range(3):
        work.arrive(t, out_ref, swap)
    for zp in range(4):
        @pl.when(zp != z)
        def _():
            sends[3 - zp].wait_send()
    net.finish()


def vm(*shape, dtype=BF16):
    return pltpu.VMEM(shape, dtype)


def dispatch(x, ids_t, gates_t, scaled, cid):
    v = pl.BlockSpec(memory_space=pltpu.VMEM)
    ws = [w for _, w in COLS]
    return pl.pallas_call(
        functools.partial(dispatch_kernel, scaled),
        out_shape=(jax.ShapeDtypeStruct((1280, D), BF16), jax.ShapeDtypeStruct((3, 4, 2, 2, 2, 16, 128), F32)),
        in_specs=[v] * 3, out_specs=(v, v),
        scratch_shapes=[vm(8, 128, w) for w in ws] + [vm(3, 4, BLK, w) for w in ws] + [vm(4, 4, BLK, w) for w in ws]
        + [vm(4, 4, BLK, w) for w in ws] + [vm(3, 4, 2, 2, 16, 128, dtype=F32), vm(1280, 1024), vm(1280, 1, dtype=F32),
                                            pltpu.SemaphoreType.DMA((120,)), pltpu.SemaphoreType.DMA((120,))],
        compiler_params=pltpu.CompilerParams(collective_id=cid, has_side_effects=True, vmem_limit_bytes=60 * 2**20),
    )(x, ids_t, gates_t)


def front(q, k, v, w, resid, gain, cot, ids_t, gates_t, cid):
    vs = pl.BlockSpec(memory_space=pltpu.VMEM)
    ws = [width for _, width in COLS]
    return pl.pallas_call(
        front_kernel,
        out_shape=(jax.ShapeDtypeStruct((128, D), F32), jax.ShapeDtypeStruct((128, D), BF16),
                   jax.ShapeDtypeStruct((1280, D), BF16), jax.ShapeDtypeStruct((3, 4, 2, 2, 2, 16, 128), F32)),
        in_specs=[vs] * 9, out_specs=(vs,) * 4,
        scratch_shapes=[vm(8, 128, w) for w in ws] + [vm(3, 4, BLK, w) for w in ws] + [vm(4, 4, BLK, w) for w in ws]
        + [vm(4, 4, BLK, w) for w in ws] + [vm(3, 4, 2, 2, 16, 128, dtype=F32), vm(1280, 1024), vm(1280, 1, dtype=F32),
           vm(4, 128, 1024), vm(8, 128, 128), vm(8, 128, 128), vm(2, 512, D), vm(4, 128, 1024), vm(4, 128, D), vm(3, 128, D),
           pltpu.SemaphoreType.DMA((150,)), pltpu.SemaphoreType.DMA((150,)), pltpu.SemaphoreType.DMA((11,))],
        compiler_params=pltpu.CompilerParams(collective_id=cid, has_side_effects=True, vmem_limit_bytes=62 * 2**20),
    )(q, k, v, w, resid, gain, cot, ids_t, gates_t)


def return_kernel(eo_ref, gi_ref, ranks, moe_ref, grad_ref, *scratch):
    (m0, m1, m2, o0, o1, o2, n0, n1, n2, part0, part1, part2, core0, core1, core2, rs0, rs1, rs2, pick, gate, send, recv, local) = scratch
    outs, mids, news = (o0, o1, o2), (m0, m1, m2), (n0, n1, n2)
    parts, cores, rss = (part0, part1, part2), (core0, core1, core2), (rs0, rs1, rs2)
    net = Net(send, recv)
    pos, core = net.pos, net.core
    net.barrier()
    swap = swap_matrix()
    srcs = (eo_ref, gi_ref)
    phase1 = {}
    for k in range(2):
        for t in range(3):
            a1, a2, a3 = ROLES[t]
            c0, w = COLS[t]
            o = outs[t].at[k]
            for g in range(4):
                if t == 0:
                    o[g] = srcs[k][g * 320:(g + 1) * 320, c0:c0 + w].reshape(4, BLK, w)
                elif t == 1:
                    got = jnp.dot(swap, srcs[k][g * 320:(g + 1) * 320, c0:c0 + w], preferred_element_type=F32).astype(BF16)
                    o[:, g] = got.reshape(4, BLK, w)
                else:
                    rows = jnp.concatenate([srcs[k][y * 320 + g * BLK:y * 320 + (g + 1) * BLK, c0:c0 + w] for y in range(4)], axis=0)
                    o[g] = jnp.dot(swap, rows, preferred_element_type=F32).astype(BF16).reshape(4, BLK, w)
            cps = []
            for d in (1, 2, 3):
                cp = net.copy(o.at[turn(pos[a3], d)], mids[t].at[k, pos[a3]], net.peer(a3, d))
                cp.start()
                cps.append(cp)
            phase1[k, t] = cps
    phase2, kept = {}, {}
    for k in range(2):
        for t in range(3):
            a1, a2, a3 = ROLES[t]
            cps = []
            kept[k, t] = []
            for i in range(4):
                a = turn(pos[a3], 4 - i)
                if i:
                    phase1[k, t][i - 1].wait_recv()
                    here = mids[t].at[k, a]
                else:
                    here = outs[t].at[k, a]
                for d in (1, 2, 3):
                    cp = net.copy(here.at[turn(pos[a2], d)], news[t].at[k, pos[a2], a], net.peer(a2, d))
                    cp.start()
                    cps.append(cp)
                keep = pltpu.make_async_copy(here.at[pos[a2]], news[t].at[k, pos[a2], a], local.at[k * 12 + t * 4 + i])
                keep.start()
                kept[k, t].append(keep)
            phase2[k, t] = cps
    phase3 = {}
    for k in range(2):
        for t in range(3):
            a1, a2, a3 = ROLES[t]
            c0, w = COLS[t]
            build_pick(ranks.at[t], core, pick, gate)
            for cp in phase2[k, t]:
                cp.wait_recv()
            for keep in kept[k, t]:
                keep.wait()
            rows = news[t][k].reshape(1280, w)
            if k == 0:
                rows = (rows.astype(F32) * gate[...]).astype(BF16)
            total = lax.dot_general(pick[...], rows, (((0,), (0,)), ((), ())), preferred_element_type=F32)
            parts[t][k] = total.astype(BF16).reshape(4, 2, 128, w)
            cp = net.copy(parts[t].at[k, :, 1 - core], cores[t].at[k], net.mate())
            cp.start()
            phase3[k, t] = cp
    phase4 = {}
    for k in range(2):
        for t in range(3):
            a1 = ROLES[t][0]
            phase3[k, t].wait_recv()
            cores[t][k] = (cores[t][k].astype(F32) + parts[t][k, :, core].astype(F32)).astype(BF16)
            cps = []
            for d in (1, 2, 3):
                cp = net.copy(cores[t].at[k, turn(pos[a1], d)], rss[t].at[k, d - 1], net.peer(a1, d))
                cp.start()
                cps.append(cp)
            phase4[k, t] = cps
    dst = (moe_ref, grad_ref)
    for k in range(2):
        for t in range(3):
            a1 = ROLES[t][0]
            c0, w = COLS[t]
            total = cores[t][k, pos[a1]].astype(F32)
            for i, cp in enumerate(phase4[k, t]):
                cp.wait_recv()
                total = total + rss[t][k, i].astype(F32)
            dst[k][:, c0:c0 + w] = total
    net.finish()


def give_back(eo, gi, ranks, cid):
    v = pl.BlockSpec(memory_space=pltpu.VMEM)
    ws = [w for _, w in COLS]
    shape = jax.ShapeDtypeStruct((128, D), F32)
    return pl.pallas_call(
        return_kernel,
        out_shape=(shape, shape) + tuple(jax.ShapeDtypeStruct((2, 4, 4, BLK, w), BF16) for w in ws),
        in_specs=[v] * 3, out_specs=(v, v) + (pl.BlockSpec(memory_space=pl.ANY),) * 3,
        scratch_shapes=[vm(2, 4, 4, BLK, w) for w in ws] + [vm(2, 4, 4, BLK, w) for w in ws]
        + [vm(2, 4, 2, 128, w) for w in ws] + [vm(2, 4, 128, w) for w in ws] + [vm(2, 3, 128, w) for w in ws]
        + [vm(1280, 1024), vm(1280, 1, dtype=F32), pltpu.SemaphoreType.DMA((200,)), pltpu.SemaphoreType.DMA((200,)),
           pltpu.SemaphoreType.DMA((24,))],
        compiler_params=pltpu.CompilerParams(collective_id=cid, has_side_effects=True, vmem_limit_bytes=63 * 2**20),
    )(eo, gi, ranks)[:2]


def norm_rows(hidden_rows, gain):
    mean_square = jnp.mean(hidden_rows * hidden_rows, axis=-1, keepdims=True)
    return hidden_rows * lax.rsqrt(mean_square + EPSILON) * gain


def silu_parts(gate_pre):
    sigmoid_value = jax.nn.sigmoid(gate_pre)
    return (gate_pre * sigmoid_value, sigmoid_value * (1.0 + gate_pre * (1.0 - sigmoid_value)))


def on_device(
    resid,
    query,
    keys,
    values,
    out_proj,
    norm_gain,
    expert_ids,
    route_gates,
    w_gate,
    w_up,
    w_down,
    cotangent,
):
    ids_t = expert_ids[0].T
    gates_t = route_gates[0].T
    gate_weight = w_gate[0]
    up_weight = w_up[0]
    down_weight = w_down[0]
    cot_rows = cotangent[0]
    hidden, normed, grad_arrived, _ = front(query[0], keys[0], values[0], out_proj, resid[0], norm_gain[None], cot_rows, ids_t, gates_t, 5)
    _, pullback = jax.vjp(lambda hidden_rows: norm_rows(hidden_rows, norm_gain), hidden)
    arrived, ranks = dispatch(normed, ids_t, gates_t, False, 6)
    gate_pre = jnp.dot(arrived, gate_weight, preferred_element_type=jnp.float32)
    up_pre = jnp.dot(arrived, up_weight, preferred_element_type=jnp.float32)
    silu_value, silu_slope = silu_parts(gate_pre)
    inner = (silu_value * up_pre).astype(jnp.bfloat16)
    expert_out = jnp.dot(inner, down_weight, preferred_element_type=jnp.float32).astype(
        jnp.bfloat16
    )
    contract_last = (((1,), (1,)), ((), ()))
    grad_inner = lax.dot_general(
        grad_arrived, down_weight, contract_last, preferred_element_type=jnp.float32
    )
    grad_gate = (grad_inner * up_pre * silu_slope).astype(jnp.bfloat16)
    grad_up = (grad_inner * silu_value).astype(jnp.bfloat16)
    grad_input = lax.dot_general(
        grad_gate, gate_weight, contract_last, preferred_element_type=jnp.float32
    )
    grad_input = grad_input + lax.dot_general(
        grad_up, up_weight, contract_last, preferred_element_type=jnp.float32
    )
    grad_input = grad_input.astype(jnp.bfloat16)
    moe_sum, normed_grad = give_back(expert_out, grad_input, ranks, 7)
    layer_out = (hidden + moe_sum).astype(jnp.bfloat16)
    grad_hidden = cot_rows.astype(jnp.float32) + pullback(normed_grad)[0]
    return (layer_out[None], grad_hidden[None])


def solution(mesh):
    placed = (
        P("ep", "cp", None),
        P("ep", "cp", None),
        P("ep", "cp", None),
        P("ep", "cp", None),
        P("cp", None),
        P(),
        P("ep", "cp", None),
        P("ep", "cp", None),
        P(("cp", "ep"), None, None),
        P(("cp", "ep"), None, None),
        P(("cp", "ep"), None, None),
        P("ep", "cp", None),
    )
    return jax.shard_map(
        on_device,
        mesh=mesh,
        in_specs=placed,
        out_specs=(P("ep", "cp", None), P("ep", "cp", None)),
        check_vma=False,
    )
```

```python
import functools
import jax
import jax.numpy as jnp
from jax import lax
from jax.experimental import pallas as pl
from jax.experimental.pallas import tpu as pltpu
from jax.sharding import PartitionSpec as P

MESH = pl.DeviceIdType.MESH
D = 2048
EPSILON = 1e-06
HEAD = 128
CAP = 10
BLK = 80
FF = 768
FRONT = ((0, 0, 768), (0, 768, 768), (1, 1536, 512))
BACK = ((0, 0, 640), (1, 640, 640), (2, 1280, 768))
ROLES = ((2, 0, 1), (0, 1, 2), (1, 2, 0))
F32 = jnp.float32
BF16 = jnp.bfloat16


def coords():
    cp = lax.axis_index("cp")
    ep = lax.axis_index("ep")
    x = lax.div(ep, 8) * 2 + lax.rem(cp, 2)
    y = lax.rem(lax.div(ep, 2), 4)
    z = lax.div(cp, 2)
    return (x, y, z), lax.rem(ep, 2)


def place(pos, core):
    x, y, z = pos
    return (z * 2 + lax.rem(x, 2), lax.div(x, 2) * 8 + y * 2 + core)


def turn(v, d):
    return lax.rem(v + d, 4)


def moved(pos, axis, d):
    return tuple(turn(p, d) if i == axis else p for i, p in enumerate(pos))


class Net:
    def __init__(self, send, recv, local):
        self.pos, self.core = coords()
        self.send, self.recv, self.here = send, recv, local
        self.count = 0
        self.local_count = 0
        self.open = []

    def peer(self, axis, d):
        return place(moved(self.pos, axis, d), self.core)

    def mate(self):
        return place(self.pos, 1 - self.core)

    def copy(self, src, dst, target):
        n = self.count
        self.count += 1
        made = pltpu.make_async_remote_copy(
            src_ref=src, dst_ref=dst, send_sem=self.send.at[n], recv_sem=self.recv.at[n],
            device_id=target, device_id_type=MESH)
        self.open.append(made)
        return made

    def local(self, src, dst):
        n = self.local_count
        self.local_count += 1
        return pltpu.make_async_copy(src, dst, self.here.at[n])

    def barrier(self, more=()):
        bar = pltpu.get_barrier_semaphore()
        targets = list(more) + [self.peer(a, d) for a in range(3) for d in (1, 2, 3)] + [self.mate()]
        for t in targets:
            pl.semaphore_signal(bar, inc=1, device_id=t, device_id_type=MESH)
        pl.semaphore_wait(bar, len(targets))

    def finish(self):
        for made in self.open:
            made.wait_send()


def swap_matrix():
    r = lax.broadcasted_iota(jnp.int32, (320, 320), 0)
    c = lax.broadcasted_iota(jnp.int32, (320, 320), 1)
    b, rest = lax.div(r, 80), lax.rem(r, 80)
    a, w = lax.div(rest, 20), lax.rem(rest, 20)
    return (c == a * 80 + b * 20 + w).astype(F32).astype(BF16)


def ranks_to(ids_ref, gates_ref, out_ref, t):
    a1, a2, a3 = ROLES[t]
    q = lax.broadcasted_iota(jnp.int32, (128, 128), 0)
    digit = {a1: lax.div(q, 32), a2: lax.rem(lax.div(q, 4), 4), a3: lax.rem(q, 4)}
    core = lax.rem(lax.div(q, 16), 2)
    e0, e1 = place((digit[0], digit[1], digit[2]), core)
    expert = e0 * 16 + e1
    named = jnp.zeros((128, 128), F32)
    gate = jnp.zeros((128, 128), F32)
    for j in range(8):
        hit = ids_ref[j:j + 1, :] == expert
        named = named + jnp.where(hit, 1.0, 0.0)
        gate = gate + jnp.where(hit, gates_ref[j:j + 1, :], 0.0)
    lo = lax.broadcasted_iota(jnp.int32, (128, 128), 0)
    hi = lax.broadcasted_iota(jnp.int32, (128, 128), 1)
    upto = (lo <= hi).astype(F32).astype(BF16)
    seen = jnp.dot(named.astype(BF16), upto, preferred_element_type=F32)
    rank = jnp.where(named > 0.5, seen - 1.0, -1000.0)
    out_ref[:, :, 0] = rank.reshape(4, 2, 16, 128)
    out_ref[:, :, 1] = gate.reshape(4, 2, 16, 128)


def build_pick(ranks, core, pick_ref, gate_ref=None):
    rows = lax.broadcasted_iota(jnp.int32, (BLK, 128), 0).astype(F32)

    def step(e, carry):
        at = pl.multiple_of(e * BLK, 16)
        total = jnp.zeros((BLK, 128), F32)
        for s in range(8):
            rank = ranks[s // 2, s % 2, core, 0, pl.ds(e, 1), :]
            hit = rank + float(CAP * s) == rows
            pick_ref[pl.ds(at, BLK), s * 128:(s + 1) * 128] = jnp.where(hit, 1.0, 0.0).astype(BF16)
            if gate_ref is not None:
                gate = ranks[s // 2, s % 2, core, 1, pl.ds(e, 1), :]
                total = total + jnp.where(hit, gate, 0.0)
        if gate_ref is not None:
            gate_ref[pl.ds(at, BLK), :] = jnp.sum(total, axis=1, keepdims=True)
        return carry
    lax.fori_loop(0, 16, step, 0)


class Ranks:
    def __init__(self, net, own_ranks, ranks):
        self.net, self.own_ranks, self.ranks = net, own_ranks, ranks
        self.sends, self.mates = [], []

    def send(self, ids_ref, gates_ref):
        net, pos, core = self.net, self.net.pos, self.net.core
        own_ranks, ranks = self.own_ranks, self.ranks
        for t in range(3):
            a1 = ROLES[t][0]
            ranks_to(ids_ref, gates_ref, own_ranks.at[t], t)
            cps = [net.copy(own_ranks.at[t, turn(pos[a1], d)], ranks.at[t, pos[a1], core], net.peer(a1, d)) for d in (1, 2, 3)]
            for cp in cps:
                cp.start()
            ranks[t, pos[a1], core] = own_ranks[t, pos[a1]]
            mate = net.copy(own_ranks.at[t, pos[a1], 1 - core], ranks.at[t, pos[a1], core, 1 - core], net.mate())
            mate.start()
            self.sends.append(cps)
            self.mates.append([mate])

    def forward(self):
        net, pos, core, ranks = self.net, self.net.pos, self.net.core, self.ranks
        for t in range(3):
            a1 = ROLES[t][0]
            for i, d in enumerate((1, 2, 3)):
                self.sends[t][i].wait_recv()
                a = turn(pos[a1], 4 - d)
                cp = net.copy(ranks.at[t, a, core, 1 - core], ranks.at[t, a, core, 1 - core], net.mate())
                cp.start()
                self.mates[t].append(cp)

    def wait(self, t):
        for cp in self.mates[t]:
            cp.wait_recv()


class Dispatch:
    def __init__(self, net, scaled, parts, ags, sels, mids, ends, ranks, pick, gate):
        self.net, self.scaled, self.parts = net, scaled, parts
        self.ags, self.sels, self.mids, self.ends = ags, sels, mids, ends
        self.ranks, self.pick, self.gate = ranks, pick, gate
        self.gathers, self.own, self.forwards, self.firsts, self.seconds = [], [], [], [], []

    def gather(self, x_ref):
        net, pos, core = self.net, self.net.pos, self.net.core
        for p, (t, c0, w) in enumerate(self.parts):
            a1 = ROLES[t][0]
            src = x_ref.at[:, c0:c0 + w]
            dst = self.ags[p].at[pos[a1], core]
            cps = [net.copy(src, dst, net.peer(a1, d)) for d in (1, 2, 3)]
            mate = net.copy(src, dst, net.mate())
            for cp in cps + [mate]:
                cp.start()
            self.gathers.append(cps)
            self.own.append(mate)
        for p, (t, c0, w) in enumerate(self.parts):
            self.ags[p][pos[ROLES[t][0]], core] = x_ref[:, c0:c0 + w]

    def forward(self, p):
        net, pos, core = self.net, self.net.pos, self.net.core
        a1 = ROLES[self.parts[p][0]][0]
        fw = []
        for i, d in enumerate((1, 2, 3)):
            self.gathers[p][i].wait_recv()
            at = self.ags[p].at[turn(pos[a1], 4 - d), core]
            cp = net.copy(at, at, net.mate())
            cp.start()
            fw.append(cp)
        self.forwards.append(fw)

    def build(self, p):
        build_pick(self.ranks.at[self.parts[p][0]], self.net.core, self.pick, self.gate if self.scaled else None)

    def select(self, p):
        net, pos = self.net, self.net.pos
        t, c0, w = self.parts[p]
        a1, a2, a3 = ROLES[t]
        self.own[p].wait_recv()
        for cp in self.forwards[p]:
            cp.wait_recv()
        sel, mid, ag = self.sels[p], self.mids[p], self.ags[p]
        cps = [net.copy(sel.at[d - 1], mid.at[pos[a2]], net.peer(a2, d)) for d in (1, 2, 3)]
        for d in (1, 2, 3, 4):
            at = pl.multiple_of(turn(pos[a2], d) * 320, 16)
            rows = jnp.dot(self.pick[pl.ds(at, 320), :], ag[...].reshape(1024, w), preferred_element_type=F32)
            if self.scaled:
                rows = rows * self.gate[pl.ds(at, 320), :]
            sel[d - 1] = rows.astype(BF16).reshape(4, BLK, w)
            if d < 4:
                cps[d - 1].start()
        self.firsts.append(cps)

    def second(self, p):
        net, pos = self.net, self.net.pos
        a1, a2, a3 = ROLES[self.parts[p][0]]
        end = self.ends[p]
        sec, kept = [], []
        for i in range(4):
            a = turn(pos[a2], 4 - i)
            if i:
                self.firsts[p][i - 1].wait_recv()
                here = self.mids[p].at[a]
            else:
                here = self.sels[p].at[3]
            for d in (1, 2, 3):
                cp = net.copy(here.at[turn(pos[a3], d)], end.at[pos[a3], a], net.peer(a3, d))
                cp.start()
                sec.append(cp)
            keep = net.local(here.at[pos[a3]], end.at[pos[a3], a])
            keep.start()
            kept.append(keep)
        self.seconds.append((sec, kept))

    def arrived(self, p):
        sec, kept = self.seconds[p]
        for cp in sec:
            cp.wait_recv()
        for keep in kept:
            keep.wait()


def front_kernel(q_ref, k_ref, v_ref, w_ref, resid_ref, gain_ref, cot_ref, ids_ref, gates_ref,
                 hidden_ref, normed_ref, out_ref, ranks_out, *scratch):
    (ag0, ag1, ag2, sel0, sel1, sel2, mid0, mid1, mid2, end2, turned,
     own_ranks, pick, gate, qbuf, kbuf, vbuf, wbuf, att, part, rs, send, recv, here, local) = scratch
    net = Net(send, recv, here)
    pos, core = net.pos, net.core
    x, y, z = pos
    side = lax.rem(x, 2)
    other = x + 1 - 2 * side
    net.barrier([place((other, y, turn(z, d)), core) for d in (1, 2, 3)])
    ranks = Ranks(net, own_ranks, ranks_out)
    ends = [out_ref.at[:, :, :, c0:c0 + w] for _, c0, w in FRONT[:2]] + [end2]
    work = Dispatch(net, True, FRONT, (ag0, ag1, ag2), (sel0, sel1, sel2), (mid0, mid1, mid2), ends, ranks_out, pick, gate)
    block = z * 2 + side

    def heads(ref, group, width):
        return ref.at[:, pl.ds(pl.multiple_of(group * width, width), width)]
    moves = []
    for d in (1, 2, 3):
        g = turn(z, d)
        moves.append(net.copy(heads(q_ref, g, 1024), qbuf.at[z], net.peer(2, d)))
    for d in (1, 2, 3, 0):
        g = turn(z, d)
        for xx in (x, other):
            if d or xx is other:
                for ref, buf in ((k_ref, kbuf), (v_ref, vbuf)):
                    moves.append(net.copy(heads(ref, g, 128), buf.at[block], place((xx, y, g), core)))
    for cp in moves:
        cp.start()
    keeps = [pltpu.make_async_copy(heads(q_ref, z, 1024), qbuf.at[z], local.at[0]),
             pltpu.make_async_copy(heads(k_ref, z, 128), kbuf.at[block], local.at[1]),
             pltpu.make_async_copy(heads(v_ref, z, 128), vbuf.at[block], local.at[2]),
             pltpu.make_async_copy(w_ref, wbuf.at[side], local.at[3])]
    for cp in keeps:
        cp.start()
    work.gather(cot_ref)
    ranks.send(ids_ref, gates_ref)
    quarters = []
    for i, d in enumerate((1, 3)):
        at = pl.ds(pl.multiple_of((core * 2 + i) * 128, 128), 128)
        cp = net.copy(w_ref.at[at], wbuf.at[side, at], net.peer(0, d))
        cp.start()
        quarters.append(cp)
    ranks.forward()
    ranks.wait(0)
    work.build(0)
    work.forward(0)
    work.forward(1)
    work.select(0)
    work.select(1)
    work.forward(2)
    ranks.wait(1)
    work.build(2)
    work.select(2)
    ranks.wait(2)
    for cp in quarters:
        cp.wait_recv()
    at = pl.ds(pl.multiple_of(core * 256, 256), 256)
    half = net.copy(wbuf.at[1 - side, at], wbuf.at[1 - side, at], net.mate())
    half.start()
    for cp in moves:
        cp.wait_recv()
    for cp in keeps:
        cp.wait()
    sends = []
    for zp in (3, 2, 1, 0):
        span = 256 * (zp + 1)

        def pair(i, carry):
            lanes = pl.multiple_of(i * 256, 256)
            two = qbuf[zp, :, pl.ds(lanes, 256)]
            rows = jnp.concatenate([two[:, :128], two[:, 128:]], axis=0)
            scores = lax.dot_general(rows, kbuf[0:2 * zp + 2].reshape(span, 128), (((1,), (1,)), ((), ())),
                                     preferred_element_type=F32) * HEAD ** (-0.5)
            row = lax.broadcasted_iota(jnp.int32, (256, span), 0)
            col = lax.broadcasted_iota(jnp.int32, (256, span), 1)
            seen = col <= lax.rem(row, 128) + (2 * zp + side) * 128
            scores = jnp.where(seen, scores, -jnp.inf)
            weights = jnp.exp(scores - jnp.max(scores, axis=1, keepdims=True))
            probs = (weights / jnp.sum(weights, axis=1, keepdims=True)).astype(BF16)
            got = jnp.dot(probs, vbuf[0:2 * zp + 2].reshape(span, 128), preferred_element_type=F32).astype(BF16)
            att[zp, :, pl.ds(lanes, 256)] = jnp.concatenate([got[:128], got[128:]], axis=1)
            return carry
        lax.fori_loop(0, 4, pair, 0)
        if zp == 3:
            half.wait_recv()

        def project(i, carry):
            lanes = pl.ds(pl.multiple_of(i * 512, 512), 512)
            total = jnp.dot(att[zp], wbuf[:, :, lanes].reshape(1024, 512), preferred_element_type=F32)
            part[zp, :, lanes] = total.astype(BF16)
            return carry
        lax.fori_loop(0, 4, project, 0)
        far = lax.rem(zp + 4 - z, 4)
        slot = lax.rem(far + 3, 4)
        cp = pltpu.make_async_remote_copy(
            src_ref=part.at[zp], dst_ref=rs.at[slot], send_sem=local.at[4 + zp], recv_sem=local.at[8 + slot],
            device_id=place((x, y, zp), core), device_id_type=MESH)

        @pl.when(zp != z)
        def _():
            cp.start()
        sends.append(cp)
    for t in range(3):
        work.second(t)
    total = resid_ref[...].astype(F32) + part[z].astype(F32)
    for d in (1, 2, 3):
        pltpu.make_async_remote_copy(
            src_ref=part.at[0], dst_ref=rs.at[d - 1], send_sem=local.at[4], recv_sem=local.at[7 + d],
            device_id=net.peer(2, d), device_id_type=MESH).wait_recv()
        total = total + rs[d - 1].astype(F32)
    hidden_ref[...] = total
    scale = lax.rsqrt(jnp.mean(total * total, axis=1, keepdims=True) + EPSILON)
    normed_ref[...] = (total * scale * gain_ref[...]).astype(BF16)
    swap = swap_matrix()
    work.arrived(2)
    c0, w = FRONT[2][1:]
    for g in range(4):
        turned[g] = jnp.dot(swap, end2[:, g].reshape(320, w), preferred_element_type=F32).astype(BF16).reshape(4, BLK, w)
    last = net.local(turned, out_ref.at[:, :, :, c0:c0 + w])
    last.start()
    work.arrived(0)
    work.arrived(1)
    last.wait()
    for zp in range(4):
        @pl.when(zp != z)
        def _():
            sends[3 - zp].wait_send()
    net.finish()


def vm(*shape, dtype=BF16):
    return pltpu.VMEM(shape, dtype)


def front(q, k, v, w, resid, gain, cot, ids_t, gates_t, cid):
    vs = pl.BlockSpec(memory_space=pltpu.VMEM)
    ws = [width for _, _, width in FRONT]
    return pl.pallas_call(
        front_kernel,
        out_shape=(jax.ShapeDtypeStruct((128, D), F32), jax.ShapeDtypeStruct((128, D), BF16),
                   jax.ShapeDtypeStruct((4, 4, BLK, D), BF16), jax.ShapeDtypeStruct((3, 4, 2, 2, 2, 16, 128), F32)),
        in_specs=[vs] * 9, out_specs=(vs, vs, pl.BlockSpec(memory_space=pl.ANY), vs),
        scratch_shapes=[vm(4, 2, 128, w) for w in ws] + [vm(4, 4, BLK, w) for w in ws] * 2
        + [vm(4, 4, BLK, ws[2])] * 2 + [vm(3, 4, 2, 2, 16, 128, dtype=F32), vm(1280, 1024), vm(1280, 1, dtype=F32),
           vm(4, 128, 1024), vm(8, 128, 128), vm(8, 128, 128), vm(2, 512, D), vm(4, 128, 1024), vm(4, 128, D), vm(3, 128, D),
           pltpu.SemaphoreType.DMA((150,)), pltpu.SemaphoreType.DMA((150,)), pltpu.SemaphoreType.DMA((20,)),
           pltpu.SemaphoreType.DMA((11,))],
        compiler_params=pltpu.CompilerParams(collective_id=cid, has_side_effects=True, vmem_limit_bytes=62 * 2**20),
    )(q, k, v, w, resid, gain, cot, ids_t, gates_t)


def back_kernel(x_ref, ranks, gin_ref, wg_ref, wu_ref, wd_ref, hidden_ref, cot_ref, gain_ref, out_ref, grad_ref, *scratch):
    (mid0, mid1, mid2, rmid0, rmid1, rmid2, new0, new1, new2,
     ag0, ag1, ag2, sel0, sel1, sel2, end0, end1, end2, pick, gate, wg, wu, wd, value, slope, inner, gup, stage, gin,
     part0, part1, part2, core0, core1, core2, rs0, rs1, rs2, send, recv, here) = scratch
    net = Net(send, recv, here)
    pos, core = net.pos, net.core
    ags, sels, ends = (ag0, ag1, ag2), (sel0, sel1, sel2), (end0, end1, end2)
    rmids, news, cores, rss = (rmid0, rmid1, rmid2), (new0, new1, new2), (core0, core1, core2), (rs0, rs1, rs2)
    loads = [net.local(a, b) for a, b in ((wg_ref, wg), (wu_ref, wu), (wd_ref, wd))]
    for cp in loads:
        cp.start()
    net.barrier()
    work = Dispatch(net, False, BACK, ags, sels, (mid0, mid1, mid2), ends, ranks, pick, None)
    work.gather(x_ref)
    work.build(0)
    for p in range(3):
        work.forward(p)
    for p in range(3):
        if p:
            work.build(p)
        work.select(p)
    for p in range(3):
        work.second(p)
    swap = swap_matrix()
    for cp in loads:
        cp.wait()

    def turned(rows):
        return jnp.dot(swap, rows, preferred_element_type=F32).astype(BF16)
    for p in range(3):
        t, c0, w = BACK[p]
        work.arrived(p)

        def pre(g, carry):
            rows = ends[p][g] if p != 1 else ends[p][:, g]
            rows = rows.reshape(320, w)
            if p:
                rows = turned(rows)
            for weight, total in ((wg, value), (wu, slope)):
                got = jnp.dot(rows, weight[c0:c0 + w, :], preferred_element_type=F32).reshape(4, BLK, FF)
                if p == 0:
                    total[g] = got
                elif p == 1:
                    total[g] += got
                else:
                    total[:, g] += got
            return carry
        lax.fori_loop(0, 4, pre, 0)

    def activate(i, carry):
        gate_pre, up_pre = value[i // 4, lax.rem(i, 4)], slope[i // 4, lax.rem(i, 4)]
        sigmoid = jax.nn.sigmoid(gate_pre)
        silu = gate_pre * sigmoid
        inner[i // 4, lax.rem(i, 4)] = (silu * up_pre).astype(BF16)
        value[i // 4, lax.rem(i, 4)] = silu
        slope[i // 4, lax.rem(i, 4)] = up_pre * (sigmoid * (1.0 + gate_pre * (1.0 - sigmoid)))
        return carry
    lax.fori_loop(0, 16, activate, 0)
    for cps in work.firsts:
        for cp in cps:
            cp.wait_send()
    for sec, _ in work.seconds:
        for i in range(3):
            sec[i].wait_send()
    done = set(id(cp) for cps in work.firsts for cp in cps) | set(id(sec[i]) for sec, _ in work.seconds for i in range(3))
    phase1, phase2, phase3, phase4 = {}, {}, {}, {}
    for fw in work.forwards:
        for cp in fw:
            cp.wait_send()
            done.add(id(cp))

    def first_back(k, p, rows_of, product):
        t, c0, w = BACK[p]
        a3 = ROLES[t][2]
        store = (sels, ends)[k][p]
        base = net.count
        cps = [net.copy(store.at[turn(pos[a3], d)], rmids[p].at[k, pos[a3]], net.peer(a3, d)) for d in (1, 2, 3)]

        def step(i, carry):
            g = turn(pos[a3], i + 1) if p != 1 else i
            got = product(rows_of(p, g), c0, w).astype(BF16).reshape(4, BLK, w)
            if p == 1:
                store[:, g] = got
            else:
                store[g] = got
                for d in (1, 2, 3):
                    @pl.when(i == d - 1)
                    def _():
                        cps[d - 1].start()
            return carry
        lax.fori_loop(0, 4, step, 0)
        if p == 1:
            for cp in cps:
                cp.start()
        phase1[k, p] = cps

    def inner_rows(ref):
        def rows(p, g):
            got = (ref[g] if p != 2 else ref[:, g]).reshape(320, FF)
            return turned(got) if p else got
        return rows
    for p in range(3):
        first_back(0, p, inner_rows(inner), lambda rows, c0, w: jnp.dot(rows, wd[:, c0:c0 + w], preferred_element_type=F32))
    nt = (((1,), (1,)), ((), ()))
    fetch = [net.local(gin_ref.at[g], gin.at[g % 2]) for g in range(4)]
    fetch[0].start()
    for g in range(4):
        if g < 3:
            fetch[g + 1].start()
        fetch[g].wait()
        grad = lax.dot_general(gin[g % 2].reshape(320, D), wd[...], nt, preferred_element_type=F32).reshape(4, BLK, FF)
        inner[g] = (grad * slope[g]).astype(BF16)
        gup[g] = (grad * value[g]).astype(BF16)
    gate_rows, up_rows = inner_rows(inner), inner_rows(gup)

    def both(rows, c0, w):
        return (lax.dot_general(rows[0], wg[c0:c0 + w, :], nt, preferred_element_type=F32)
                + lax.dot_general(rows[1], wu[c0:c0 + w, :], nt, preferred_element_type=F32))
    for p in range(3):
        first_back(1, p, lambda p, g: (gate_rows(p, g), up_rows(p, g)), both)
    for k in range(2):
        for p in range(3):
            a1, a2, a3 = ROLES[BACK[p][0]]
            cps, kept = [], []
            for i in range(4):
                a = turn(pos[a3], 4 - i)
                if i:
                    phase1[k, p][i - 1].wait_recv()
                    at = rmids[p].at[k, a]
                else:
                    at = (sels, ends)[k][p].at[a]
                for d in (1, 2, 3):
                    cp = net.copy(at.at[turn(pos[a2], d)], news[p].at[k, pos[a2], a], net.peer(a2, d))
                    cp.start()
                    cps.append(cp)
                keep = net.local(at.at[pos[a2]], news[p].at[k, pos[a2], a])
                keep.start()
                kept.append(keep)
            phase2[k, p] = cps, kept
    parts = (ags, (part0, part1, part2))

    def pass_on(k, p):
        a1 = ROLES[BACK[p][0]][0]
        phase3[k, p].wait_recv()
        cores[p][k] = (cores[p][k].astype(F32) + parts[k][p][:, core].astype(F32)).astype(BF16)
        cps = [net.copy(cores[p].at[k, turn(pos[a1], d)], rss[p].at[k, d - 1], net.peer(a1, d)) for d in (1, 2, 3)]
        for cp in cps:
            cp.start()
        phase4[k, p] = cps
    order = [(k, p) for k in range(2) for p in range(3)]
    for n, (k, p) in enumerate(order):
        t, c0, w = BACK[p]
        build_pick(ranks.at[t], core, pick, gate)
        cps, kept = phase2[k, p]
        for cp in cps:
            cp.wait_recv()
        for keep in kept:
            keep.wait()
        load = net.local(news[p].at[k], stage.at[:, :, :, :w])
        load.start()
        load.wait()
        rows = stage[:, :, :, :w].reshape(1280, w)
        if k == 0:
            rows = (rows.astype(F32) * gate[...]).astype(BF16)
        total = lax.dot_general(pick[...], rows, (((0,), (0,)), ((), ())), preferred_element_type=F32)
        parts[k][p][...] = total.astype(BF16).reshape(4, 2, 128, w)
        cp = net.copy(parts[k][p].at[:, 1 - core], cores[p].at[k], net.mate())
        cp.start()
        phase3[k, p] = cp
        if n:
            pass_on(*order[n - 1])
    pass_on(*order[-1])

    def result(k, p):
        a1 = ROLES[BACK[p][0]][0]
        total = cores[p][k, pos[a1]].astype(F32)
        for i, cp in enumerate(phase4[k, p]):
            cp.wait_recv()
            total = total + rss[p][k, i].astype(F32)
        return total
    for p in range(3):
        c0, w = BACK[p][1:]
        out_ref[:, c0:c0 + w] = (hidden_ref[:, c0:c0 + w] + result(0, p)).astype(BF16)
    for p in range(3):
        c0, w = BACK[p][1:]
        grad_ref[:, c0:c0 + w] = result(1, p) * gain_ref[:, c0:c0 + w]
    hidden = hidden_ref[...]
    scaled = grad_ref[...]
    scale = lax.rsqrt(jnp.mean(hidden * hidden, axis=1, keepdims=True) + EPSILON)
    along = jnp.mean(scaled * hidden, axis=1, keepdims=True)
    grad_ref[...] = cot_ref[...].astype(F32) + scale * scaled - hidden * (scale * scale * scale * along)
    for made in net.open:
        if id(made) not in done:
            made.wait_send()


def back(x, ranks, gin, wg, wu, wd, hidden, cot, gain, cid):
    vs = pl.BlockSpec(memory_space=pltpu.VMEM)
    anyspace = pl.BlockSpec(memory_space=pl.ANY)
    ws = [width for _, _, width in BACK]
    rows = [(4, 4, BLK, w) for w in ws]
    return pl.pallas_call(
        back_kernel,
        out_shape=(jax.ShapeDtypeStruct((128, D), BF16), jax.ShapeDtypeStruct((128, D), F32))
        + tuple(jax.ShapeDtypeStruct(r, BF16) for r in rows) + tuple(jax.ShapeDtypeStruct((2,) + r, BF16) for r in rows) * 2,
        in_specs=[vs, vs] + [anyspace] * 4 + [vs] * 3, out_specs=(vs, vs) + (anyspace,) * 9,
        scratch_shapes=[vm(4, 2, 128, w) for w in ws] + [vm(*r) for r in rows] * 2
        + [vm(1280, 1024), vm(1280, 1, dtype=F32), vm(D, FF), vm(D, FF), vm(FF, D),
           vm(4, 4, BLK, FF, dtype=F32), vm(4, 4, BLK, FF, dtype=F32), vm(4, 4, BLK, FF), vm(4, 4, BLK, FF),
           vm(4, 4, BLK, max(ws)), vm(2, 4, BLK, D)]
        + [vm(4, 2, 128, w) for w in ws] + [vm(2, 4, 128, w) for w in ws] + [vm(2, 3, 128, w) for w in ws]
        + [pltpu.SemaphoreType.DMA((220,)), pltpu.SemaphoreType.DMA((220,)), pltpu.SemaphoreType.DMA((60,))],
        compiler_params=pltpu.CompilerParams(collective_id=cid, has_side_effects=True, vmem_limit_bytes=63 * 2**20),
    )(x, ranks, gin, wg, wu, wd, hidden, cot, gain)[:2]


def on_device(
    resid,
    query,
    keys,
    values,
    out_proj,
    norm_gain,
    expert_ids,
    route_gates,
    w_gate,
    w_up,
    w_down,
    cotangent,
):
    ids_t = expert_ids[0].T
    gates_t = route_gates[0].T
    gain = norm_gain[None]
    hidden, normed, grad_arrived, ranks = front(
        query[0], keys[0], values[0], out_proj, resid[0], gain, cotangent[0], ids_t, gates_t, 5)
    layer_out, grad_hidden = back(
        normed, ranks, grad_arrived, w_gate[0], w_up[0], w_down[0], hidden, cotangent[0], gain, 6)
    return (layer_out[None], grad_hidden[None])


def solution(mesh):
    placed = (
        P("ep", "cp", None),
        P("ep", "cp", None),
        P("ep", "cp", None),
        P("ep", "cp", None),
        P("cp", None),
        P(),
        P("ep", "cp", None),
        P("ep", "cp", None),
        P(("cp", "ep"), None, None),
        P(("cp", "ep"), None, None),
        P(("cp", "ep"), None, None),
        P("ep", "cp", None),
    )
    return jax.shard_map(
        on_device,
        mesh=mesh,
        in_specs=placed,
        out_specs=(P("ep", "cp", None), P("ep", "cp", None)),
        check_vma=False,
    )
```

```python
import functools
import jax
import jax.numpy as jnp
from jax import lax
from jax.experimental import pallas as pl
from jax.experimental.pallas import tpu as pltpu
from jax.sharding import PartitionSpec as P

MESH = pl.DeviceIdType.MESH
D = 2048
EPSILON = 1e-06
HEAD = 128
CAP = 10
BLK = 80
FF = 768
FRONT = ((0, 0, 512), (3, 512, 512), (0, 1024, 512), (3, 1536, 512))
BACK = ((0, 0, 640), (1, 640, 640), (2, 1280, 768))
ROLES = ((2, 0, 1), (0, 1, 2), (1, 2, 0), (2, 1, 0))
F32 = jnp.float32
BF16 = jnp.bfloat16


def coords():
    cp = lax.axis_index("cp")
    ep = lax.axis_index("ep")
    x = lax.div(ep, 8) * 2 + lax.rem(cp, 2)
    y = lax.rem(lax.div(ep, 2), 4)
    z = lax.div(cp, 2)
    return (x, y, z), lax.rem(ep, 2)


def place(pos, core):
    x, y, z = pos
    return (z * 2 + lax.rem(x, 2), lax.div(x, 2) * 8 + y * 2 + core)


def turn(v, d):
    return lax.rem(v + d, 4)


def moved(pos, axis, d):
    return tuple(turn(p, d) if i == axis else p for i, p in enumerate(pos))


class Net:
    def __init__(self, send, recv, local):
        self.pos, self.core = coords()
        self.send, self.recv, self.here = send, recv, local
        self.count = 0
        self.local_count = 0
        self.open = []

    def peer(self, axis, d):
        return place(moved(self.pos, axis, d), self.core)

    def mate(self):
        return place(self.pos, 1 - self.core)

    def copy(self, src, dst, target):
        n = self.count
        self.count += 1
        made = pltpu.make_async_remote_copy(
            src_ref=src, dst_ref=dst, send_sem=self.send.at[n], recv_sem=self.recv.at[n],
            device_id=target, device_id_type=MESH)
        self.open.append(made)
        return made

    def local(self, src, dst):
        n = self.local_count
        self.local_count += 1
        return pltpu.make_async_copy(src, dst, self.here.at[n])

    def greet(self, more=()):
        bar = pltpu.get_barrier_semaphore()
        self.targets = targets = list(more) + [self.peer(a, d) for a in range(3) for d in (1, 2, 3)] + [self.mate()]
        for t in targets:
            pl.semaphore_signal(bar, inc=1, device_id=t, device_id_type=MESH)

    def meet(self):
        pl.semaphore_wait(pltpu.get_barrier_semaphore(), len(self.targets))

    def finish(self):
        for made in self.open:
            made.wait_send()


def swap_matrix():
    r = lax.broadcasted_iota(jnp.int32, (320, 320), 0)
    c = lax.broadcasted_iota(jnp.int32, (320, 320), 1)
    b, rest = lax.div(r, 80), lax.rem(r, 80)
    a, w = lax.div(rest, 20), lax.rem(rest, 20)
    return (c == a * 80 + b * 20 + w).astype(F32).astype(BF16)


def ranks_to(ids_ref, gates_ref, out_ref, t):
    a1, a2, a3 = ROLES[t]
    q = lax.broadcasted_iota(jnp.int32, (128, 128), 0)
    digit = {a1: lax.div(q, 32), a2: lax.rem(lax.div(q, 4), 4), a3: lax.rem(q, 4)}
    core = lax.rem(lax.div(q, 16), 2)
    e0, e1 = place((digit[0], digit[1], digit[2]), core)
    expert = e0 * 16 + e1
    named = jnp.zeros((128, 128), F32)
    gate = jnp.zeros((128, 128), F32)
    for j in range(8):
        hit = ids_ref[j:j + 1, :] == expert
        named = named + jnp.where(hit, 1.0, 0.0)
        gate = gate + jnp.where(hit, gates_ref[j:j + 1, :], 0.0)
    lo = lax.broadcasted_iota(jnp.int32, (128, 128), 0)
    hi = lax.broadcasted_iota(jnp.int32, (128, 128), 1)
    upto = (lo <= hi).astype(F32).astype(BF16)
    seen = jnp.dot(named.astype(BF16), upto, preferred_element_type=F32)
    rank = jnp.where(named > 0.5, seen - 1.0, -1000.0)
    out_ref[:, :, 0] = rank.reshape(4, 2, 16, 128)
    out_ref[:, :, 1] = gate.reshape(4, 2, 16, 128)


def build_pick(ranks, core, pick_ref, gate_ref=None):
    rows = lax.broadcasted_iota(jnp.int32, (BLK, 128), 0).astype(F32)

    def step(e, carry):
        u, v = lax.div(e, 4), lax.rem(e, 4)
        total = jnp.zeros((BLK, 128), F32)
        for s in range(8):
            rank = ranks[s // 2, s % 2, core, 0, pl.ds(e, 1), :]
            hit = rank + float(CAP * s) == rows
            pick_ref[u, v, :, s * 128:(s + 1) * 128] = jnp.where(hit, 1.0, 0.0).astype(BF16)
            if gate_ref is not None:
                gate = ranks[s // 2, s % 2, core, 1, pl.ds(e, 1), :]
                total = total + jnp.where(hit, gate, 0.0)
        if gate_ref is not None:
            gate_ref[u, v] = jnp.sum(total, axis=1, keepdims=True)
        return carry
    lax.fori_loop(0, 16, step, 0)


class Ranks:
    def __init__(self, net, own_ranks, ranks):
        self.net, self.own_ranks, self.ranks = net, own_ranks, ranks
        self.sends, self.mates = [], []

    def prepare(self, ids_ref, gates_ref):
        for t in range(3):
            ranks_to(ids_ref, gates_ref, self.own_ranks.at[t], t)

    def send(self):
        net, pos, core = self.net, self.net.pos, self.net.core
        own_ranks, ranks = self.own_ranks, self.ranks
        for t in range(3):
            a1 = ROLES[t][0]
            cps = [net.copy(own_ranks.at[t, turn(pos[a1], d)], ranks.at[t, pos[a1], core], net.peer(a1, d)) for d in (1, 2, 3)]
            for cp in cps:
                cp.start()
            ranks[t, pos[a1], core] = own_ranks[t, pos[a1]]
            mate = net.copy(own_ranks.at[t, pos[a1], 1 - core], ranks.at[t, pos[a1], core, 1 - core], net.mate())
            mate.start()
            self.sends.append(cps)
            self.mates.append([mate])

    def forward(self):
        net, pos, core, ranks = self.net, self.net.pos, self.net.core, self.ranks
        for t in range(3):
            a1 = ROLES[t][0]
            for i, d in enumerate((1, 2, 3)):
                self.sends[t][i].wait_recv()
                a = turn(pos[a1], 4 - d)
                cp = net.copy(ranks.at[t, a, core, 1 - core], ranks.at[t, a, core, 1 - core], net.mate())
                cp.start()
                self.mates[t].append(cp)

    def wait(self, t):
        for cp in self.mates[t]:
            cp.wait_recv()


class Dispatch:
    def __init__(self, net, scaled, parts, ags, sels, mids, ends, ranks, pick, gate):
        self.net, self.scaled, self.parts = net, scaled, parts
        self.ags, self.sels, self.mids, self.ends = ags, sels, mids, ends
        self.ranks, self.pick, self.gate = ranks, pick, gate
        self.gathers, self.keeps, self.forwards, self.firsts, self.seconds = {}, {}, {}, {}, {}

    def gather(self, x_ref, which):
        net, pos, core = self.net, self.net.pos, self.net.core
        for p in which:
            t, c0, w = self.parts[p]
            a1 = ROLES[t][0]
            src = x_ref.at[:, c0:c0 + w]
            dst = self.ags[p].at[pos[a1], core]
            self.gathers[p] = [net.copy(src, dst, net.peer(a1, d)) for d in (1, 2, 3)]
            self.forwards[p] = [net.copy(src, dst, net.mate())]
            self.keeps[p] = [net.local(src, dst)]
            for cp in self.gathers[p] + self.forwards[p] + self.keeps[p]:
                cp.start()

    def forward(self, p):
        net, pos, core = self.net, self.net.pos, self.net.core
        a1 = ROLES[self.parts[p][0]][0]
        for i, d in enumerate((1, 2, 3)):
            self.gathers[p][i].wait_recv()
            at = self.ags[p].at[turn(pos[a1], 4 - d), core]
            cp = net.copy(at, at, net.mate())
            cp.start()
            self.forwards[p].append(cp)

    def gathered(self, p):
        for cp in self.forwards.get(p, ()):
            cp.wait_recv()
        for keep in self.keeps[p]:
            keep.wait()

    def build(self, p):
        build_pick(self.ranks.at[self.parts[p][0] % 3], self.net.core, self.pick, self.gate if self.scaled else None)

    def select(self, p):
        net, pos = self.net, self.net.pos
        t, c0, w = self.parts[p]
        a1, a2, a3 = ROLES[t]
        sel, mid, ag = self.sels[p], self.mids[p], self.ags[p]
        cps = [net.copy(sel.at[d - 1], mid.at[pos[a2]], net.peer(a2, d)) for d in (1, 2, 3)]
        for d in (1, 2, 3, 4):
            b = turn(pos[a2], d)
            mine = (lambda ref: ref[:, b]) if t == 3 else (lambda ref: ref[b])
            rows = jnp.dot(mine(self.pick).reshape(320, 1024), ag[...].reshape(1024, w), preferred_element_type=F32)
            if self.scaled:
                rows = rows * mine(self.gate).reshape(320, 1)
            sel[d - 1] = rows.astype(BF16).reshape(4, BLK, w)
            if d < 4:
                cps[d - 1].start()
        self.firsts[p] = cps

    def settle(self, p):
        keep = self.net.local(self.sels[p].at[3], self.mids[p].at[self.net.pos[ROLES[self.parts[p][0]][1]]])
        keep.start()
        for cp in self.firsts[p]:
            cp.wait_recv()
        keep.wait()

    def second(self, p):
        net, pos = self.net, self.net.pos
        t, c0, w = self.parts[p]
        a1, a2, a3 = ROLES[t]
        end = self.ends[p]
        sec, kept = [], []
        for i in range(4):
            a = turn(pos[a2], 4 - i)
            here = self.mids[p].at[a]
            if p in self.firsts:
                if i:
                    self.firsts[p][i - 1].wait_recv()
                else:
                    here = self.sels[p].at[3]
            at = end.at[(a, pos[a3]) if t == 3 else (pos[a3], a)]
            for d in (1, 2, 3):
                cp = net.copy(here.at[turn(pos[a3], d)], at, net.peer(a3, d))
                cp.start()
                sec.append(cp)
            keep = net.local(here.at[pos[a3]], at)
            keep.start()
            kept.append(keep)
        self.seconds[p] = sec, kept

    def arrived(self, p):
        sec, kept = self.seconds[p]
        for cp in sec:
            cp.wait_recv()
        for keep in kept:
            keep.wait()


def front_kernel(q_ref, k_ref, v_ref, w_ref, resid_ref, gain_ref, cot_ref, ids_ref, gates_ref,
                 hidden_ref, out_ref, mid2, mid3, next0, next1, next2, ranks_out, *scratch):
    (ag0, ag1, ag2, ag3, sel0, sel1, sel2, sel3, mid0, mid1, normed, own_ranks, pick, gate, qbuf, kbuf, vbuf, wbuf, att, part, rs, send, recv, here, local) = scratch
    net = Net(send, recv, here)
    pos, core = net.pos, net.core
    x, y, z = pos
    side = lax.rem(x, 2)
    other = x + 1 - 2 * side
    net.greet()
    ranks = Ranks(net, own_ranks, ranks_out)
    ranks.prepare(ids_ref, gates_ref)
    net.meet()
    ends = [out_ref.at[:, :, :, c0:c0 + w] for _, c0, w in FRONT[:2]] + [None, None]
    work = Dispatch(net, True, FRONT, (ag0, ag1, ag2, ag3), (sel0, sel1, sel2, sel3), (mid0, mid1, mid2, mid3), ends,
                    ranks_out, pick, gate)
    block = z * 2 + side

    def heads(ref, group, width):
        return ref.at[:, pl.ds(pl.multiple_of(group * width, width), width)]
    moves = []
    for d in (1, 2, 3):
        g = turn(z, d)
        moves.append(net.copy(heads(q_ref, g, 1024), qbuf.at[z], net.peer(2, d)))
    pairs = ((k_ref, kbuf), (v_ref, vbuf))
    kv = {d: [net.copy(heads(ref, turn(z, d), 128), buf.at[block], net.peer(2, d)) for ref, buf in pairs] for d in (1, 2, 3)}
    kv[0] = [net.copy(heads(ref, z, 128), buf.at[block], place((other, y, z), core)) for ref, buf in pairs]
    for d in (2, 1, 3, 0):
        for cp in kv[d]:
            cp.start()
    for cp in moves:
        cp.start()
    keeps = [pltpu.make_async_copy(heads(q_ref, z, 1024), qbuf.at[z], local.at[0]),
             pltpu.make_async_copy(heads(k_ref, z, 128), kbuf.at[block], local.at[1]),
             pltpu.make_async_copy(heads(v_ref, z, 128), vbuf.at[block], local.at[2]),
             pltpu.make_async_copy(w_ref, wbuf.at[side], local.at[3])]
    for cp in keeps:
        cp.start()
    ranks.send()
    work.gather(cot_ref, (0, 1))
    quarters = []
    for i, d in enumerate((1, 3)):
        at = pl.ds(pl.multiple_of((core * 2 + i) * 128, 128), 128)
        cp = net.copy(w_ref.at[at], wbuf.at[side, at], net.peer(0, d))
        cp.start()
        quarters.append(cp)
    for d in (1, 2, 3):
        for cp, (ref, buf) in zip(kv[d], pairs):
            cp.wait_recv()
            at = buf.at[turn(z, 4 - d) * 2 + side]
            on = net.copy(at, at, place((other, y, z), core))
            on.start()
            kv[0].append(on)
    ranks.forward()
    ranks.wait(0)
    work.build(0)
    for p in (0, 1):
        work.forward(p)
    work.gather(cot_ref, (2, 3))
    for p in (0, 1):
        work.gathered(p)
        work.select(p)
    ranks.wait(1)
    ranks.wait(2)
    for cp in quarters:
        cp.wait_recv()
    at = pl.ds(pl.multiple_of(core * 256, 256), 256)
    half = net.copy(wbuf.at[1 - side, at], wbuf.at[1 - side, at], net.mate())
    half.start()
    for cp in moves + kv[0]:
        cp.wait_recv()
    for cp in keeps:
        cp.wait()
    half.wait_recv()

    def attend(zp):
        span = 256 * (zp + 1)

        def pair(i, carry):
            lanes = pl.multiple_of(i * 256, 256)
            two = qbuf[zp, :, pl.ds(lanes, 256)]
            rows = jnp.concatenate([two[:, :128], two[:, 128:]], axis=0)
            scores = lax.dot_general(rows, kbuf[0:2 * zp + 2].reshape(span, 128), (((1,), (1,)), ((), ())),
                                     preferred_element_type=F32) * HEAD ** (-0.5)
            row = lax.broadcasted_iota(jnp.int32, (256, span), 0)
            col = lax.broadcasted_iota(jnp.int32, (256, span), 1)
            seen = col <= lax.rem(row, 128) + (2 * zp + side) * 128
            scores = jnp.where(seen, scores, -jnp.inf)
            weights = jnp.exp(scores - jnp.max(scores, axis=1, keepdims=True))
            probs = (weights / jnp.sum(weights, axis=1, keepdims=True)).astype(BF16)
            got = jnp.dot(probs, vbuf[0:2 * zp + 2].reshape(span, 128), preferred_element_type=F32).astype(BF16)
            att[zp, :, pl.ds(lanes, 256)] = jnp.concatenate([got[:128], got[128:]], axis=1)
            return carry
        lax.fori_loop(0, 4, pair, 0)

    def project(zp):
        def step(i, carry):
            lanes = pl.ds(pl.multiple_of(i * 512, 512), 512)
            total = jnp.dot(att[zp], wbuf[:, :, lanes].reshape(1024, 512), preferred_element_type=F32)
            part[zp, :, lanes] = total.astype(BF16)
            return carry
        lax.fori_loop(0, 4, step, 0)
    sends = {d: net.copy(part.at[turn(z, d)], rs.at[d - 1], net.peer(2, d)) for d in (2, 1, 3)}

    def turns(ds):
        def step(i, carry):
            far = ds[0] + i * (ds[1] - ds[0])
            zp = turn(z, far)
            for n in range(4):
                @pl.when(zp == n)
                def _():
                    attend(n)
            project(zp)
            for n, d in enumerate(ds):
                if d:
                    @pl.when(i == n)
                    def _():
                        sends[d].start()
            return carry
        lax.fori_loop(0, 2, step, 0)
    turns((2, 1))
    work.forward(2)
    work.forward(3)
    work.gathered(2)
    work.select(2)
    turns((3, 0))
    work.gathered(3)
    work.select(3)
    for p in range(2):
        work.second(p)
    total = resid_ref[...].astype(F32) + part[z].astype(F32)
    for d in (1, 2, 3):
        sends[d].wait_recv()
        total = total + rs[d - 1].astype(F32)
    hidden_ref[...] = total
    scale = lax.rsqrt(jnp.mean(total * total, axis=1, keepdims=True) + EPSILON)
    normed[...] = (total * scale * gain_ref[...]).astype(BF16)
    later = Dispatch(net, False, BACK, (next0, next1, next2), None, None, None, ranks_out, None, None)
    later.gather(normed, (0, 1, 2))
    for p in range(3):
        later.forward(p)
    for p in range(2):
        work.arrived(p)
    for p in (2, 3):
        work.settle(p)
    for p in range(3):
        later.gathered(p)
    net.finish()


def vm(*shape, dtype=BF16):
    return pltpu.VMEM(shape, dtype)


def front(q, k, v, w, resid, gain, cot, ids_t, gates_t, cid):
    vs = pl.BlockSpec(memory_space=pltpu.VMEM)
    anyspace = pl.BlockSpec(memory_space=pl.ANY)
    ws = [width for _, _, width in FRONT]
    half = ws[0] + ws[1]
    shapes = [(4, 4, BLK, half)] + [(4, 4, BLK, w) for w in ws[2:]] + [(4, 2, 128, w) for _, _, w in BACK]
    return pl.pallas_call(
        front_kernel,
        out_shape=(jax.ShapeDtypeStruct((128, D), F32),) + tuple(jax.ShapeDtypeStruct(r, BF16) for r in shapes)
        + (jax.ShapeDtypeStruct((3, 4, 2, 2, 2, 16, 128), F32),),
        in_specs=[anyspace] * 4 + [vs] * 5, out_specs=(vs,) + (anyspace,) * len(shapes) + (vs,),
        scratch_shapes=[vm(4, 2, 128, w) for w in ws] + [vm(4, 4, BLK, w) for w in ws] + [vm(4, 4, BLK, w) for w in ws[:2]]
        + [vm(128, D), vm(3, 4, 2, 2, 16, 128, dtype=F32), vm(4, 4, BLK, 1024), vm(4, 4, BLK, 1, dtype=F32),
           vm(4, 128, 1024), vm(8, 128, 128), vm(8, 128, 128), vm(2, 512, D), vm(4, 128, 1024), vm(4, 128, D), vm(3, 128, D),
           pltpu.SemaphoreType.DMA((180,)), pltpu.SemaphoreType.DMA((180,)), pltpu.SemaphoreType.DMA((30,)),
           pltpu.SemaphoreType.DMA((11,))],
        compiler_params=pltpu.CompilerParams(collective_id=cid, has_side_effects=True, vmem_limit_bytes=62 * 2**20),
    )(q, k, v, w, resid, gain, cot, ids_t, gates_t)


def back_kernel(next0, next1, next2, ranks, gin_ref, fmid2, fmid3, wg_ref, wu_ref, wd_ref, hidden_ref, cot_ref, gain_ref, out_ref, grad_ref, *scratch):
    (gin2, mid0, mid1, mid2, rmid0, rmid1, rmid2, new0, new1, new2,
     ag0, ag1, ag2, sel0, sel1, sel2, end0, end1, end2, pick, gate, wg, wu, wd, value, slope, inner, gup, stage, gin,
     part0, part1, part2, core0, core1, core2, rs0, rs1, rs2, send, recv, here) = scratch
    net = Net(send, recv, here)
    pos, core = net.pos, net.core
    ags, sels, ends = (ag0, ag1, ag2), (sel0, sel1, sel2), (end0, end1, end2)
    rmids, news, cores, rss = (rmid0, rmid1, rmid2), (new0, new1, new2), (core0, core1, core2), (rs0, rs1, rs2)
    loads = [net.local(a, b) for a, b in ((wg_ref, wg), (wu_ref, wu), (wd_ref, wd))]
    for cp in loads:
        cp.start()
    net.greet()
    work = Dispatch(net, False, BACK, ags, sels, (mid0, mid1, mid2), ends, ranks, pick, None)
    for p, ref in enumerate((next0, next1, next2)):
        work.keeps[p] = [net.local(ref, ags[p])]
        work.keeps[p][0].start()
    work.build(0)
    net.meet()
    for p in range(3):
        if p:
            work.build(p)
        work.gathered(p)
        work.select(p)
    for p in range(3):
        work.second(p)
    rest = Dispatch(net, True, FRONT[2:], None, None, (fmid2, fmid3),
                    [gin2.at[:, :, :, c:c + w] for c, w in ((0, FRONT[2][2]), (FRONT[2][2], FRONT[3][2]))], None, None, None)
    for p in range(2):
        rest.second(p)
    swap = swap_matrix()
    for cp in loads:
        cp.wait()

    def turned(rows):
        return jnp.dot(swap, rows, preferred_element_type=F32).astype(BF16)
    for p in range(3):
        t, c0, w = BACK[p]
        work.arrived(p)

        def pre(g, carry):
            rows = ends[p][g] if p != 1 else ends[p][:, g]
            rows = rows.reshape(320, w)
            if p:
                rows = turned(rows)
            for weight, total in ((wg, value), (wu, slope)):
                got = jnp.dot(rows, weight[c0:c0 + w, :], preferred_element_type=F32).reshape(4, BLK, FF)
                if p == 0:
                    total[g] = got
                elif p == 1:
                    total[g] += got
                else:
                    total[:, g] += got
            return carry
        lax.fori_loop(0, 4, pre, 0)

    def activate(i, carry):
        gate_pre, up_pre = value[i // 4, lax.rem(i, 4)], slope[i // 4, lax.rem(i, 4)]
        sigmoid = jax.nn.sigmoid(gate_pre)
        silu = gate_pre * sigmoid
        inner[i // 4, lax.rem(i, 4)] = (silu * up_pre).astype(BF16)
        value[i // 4, lax.rem(i, 4)] = silu
        slope[i // 4, lax.rem(i, 4)] = up_pre * (sigmoid * (1.0 + gate_pre * (1.0 - sigmoid)))
        return carry
    lax.fori_loop(0, 16, activate, 0)
    for cps in work.firsts.values():
        for cp in cps:
            cp.wait_send()
    for sec, _ in work.seconds.values():
        for i in range(3):
            sec[i].wait_send()
    done = set(id(cp) for cps in work.firsts.values() for cp in cps) | set(id(sec[i]) for sec, _ in work.seconds.values() for i in range(3))
    phase1, phase2, phase3, phase4 = {}, {}, {}, {}

    def first_back(k, p, rows_of, product):
        t, c0, w = BACK[p]
        a3 = ROLES[t][2]
        store = (sels, ends)[k][p]
        base = net.count
        cps = [net.copy(store.at[turn(pos[a3], d)], rmids[p].at[k, pos[a3]], net.peer(a3, d)) for d in (1, 2, 3)]

        def step(i, carry):
            g = turn(pos[a3], i + 1) if p != 1 else i
            got = product(rows_of(p, g), c0, w).astype(BF16).reshape(4, BLK, w)
            if p == 1:
                store[:, g] = got
            else:
                store[g] = got
                for d in (1, 2, 3):
                    @pl.when(i == d - 1)
                    def _():
                        cps[d - 1].start()
            return carry
        lax.fori_loop(0, 4, step, 0)
        if p == 1:
            for cp in cps:
                cp.start()
        phase1[k, p] = cps

    def inner_rows(ref):
        def rows(p, g):
            got = (ref[g] if p != 2 else ref[:, g]).reshape(320, FF)
            return turned(got) if p else got
        return rows
    for p in range(3):
        first_back(0, p, inner_rows(inner), lambda rows, c0, w: jnp.dot(rows, wd[:, c0:c0 + w], preferred_element_type=F32))
    nt = (((1,), (1,)), ((), ()))
    half = FRONT[2][1]
    fetch = [(net.local(gin_ref.at[g], gin.at[g % 2, :, :, :half]), net.local(gin2.at[g], gin.at[g % 2, :, :, half:])) for g in range(4)]
    for p in range(2):
        rest.arrived(p)
    for cp in fetch[0]:
        cp.start()
    for g in range(4):
        if g < 3:
            for cp in fetch[g + 1]:
                cp.start()
        for cp in fetch[g]:
            cp.wait()
        grad = lax.dot_general(gin[g % 2].reshape(320, D), wd[...], nt, preferred_element_type=F32).reshape(4, BLK, FF)
        inner[g] = (grad * slope[g]).astype(BF16)
        gup[g] = (grad * value[g]).astype(BF16)
    gate_rows, up_rows = inner_rows(inner), inner_rows(gup)

    def both(rows, c0, w):
        return (lax.dot_general(rows[0], wg[c0:c0 + w, :], nt, preferred_element_type=F32)
                + lax.dot_general(rows[1], wu[c0:c0 + w, :], nt, preferred_element_type=F32))
    for p in range(3):
        first_back(1, p, lambda p, g: (gate_rows(p, g), up_rows(p, g)), both)
    for k in range(2):
        for p in range(3):
            a1, a2, a3 = ROLES[BACK[p][0]]
            cps, kept = [], []
            for i in range(4):
                a = turn(pos[a3], 4 - i)
                if i:
                    phase1[k, p][i - 1].wait_recv()
                    at = rmids[p].at[k, a]
                else:
                    at = (sels, ends)[k][p].at[a]
                for d in (1, 2, 3):
                    cp = net.copy(at.at[turn(pos[a2], d)], news[p].at[k, pos[a2], a], net.peer(a2, d))
                    cp.start()
                    cps.append(cp)
                keep = net.local(at.at[pos[a2]], news[p].at[k, pos[a2], a])
                keep.start()
                kept.append(keep)
            phase2[k, p] = cps, kept
    parts = (ags, (part0, part1, part2))

    def pass_on(k, p):
        a1 = ROLES[BACK[p][0]][0]
        phase3[k, p].wait_recv()
        cores[p][k] = (cores[p][k].astype(F32) + parts[k][p][:, core].astype(F32)).astype(BF16)
        cps = [net.copy(cores[p].at[k, turn(pos[a1], d)], rss[p].at[k, d - 1], net.peer(a1, d)) for d in (1, 2, 3)]
        for cp in cps:
            cp.start()
        phase4[k, p] = cps
    order = [(k, p) for k in range(2) for p in range(3)]
    for n, (k, p) in enumerate(order):
        t, c0, w = BACK[p]
        build_pick(ranks.at[t], core, pick, gate)
        cps, kept = phase2[k, p]
        for cp in cps:
            cp.wait_recv()
        for keep in kept:
            keep.wait()
        load = net.local(news[p].at[k], stage.at[:, :, :, :w])
        load.start()
        load.wait()
        rows = stage[:, :, :, :w].reshape(1280, w)
        if k == 0:
            rows = (rows.astype(F32) * gate[...].reshape(1280, 1)).astype(BF16)
        total = lax.dot_general(pick[...].reshape(1280, 1024), rows, (((0,), (0,)), ((), ())), preferred_element_type=F32)
        parts[k][p][...] = total.astype(BF16).reshape(4, 2, 128, w)
        cp = net.copy(parts[k][p].at[:, 1 - core], cores[p].at[k], net.mate())
        cp.start()
        phase3[k, p] = cp
        if n:
            pass_on(*order[n - 1])
    pass_on(*order[-1])

    def result(k, p):
        a1 = ROLES[BACK[p][0]][0]
        total = cores[p][k, pos[a1]].astype(F32)
        for i, cp in enumerate(phase4[k, p]):
            cp.wait_recv()
            total = total + rss[p][k, i].astype(F32)
        return total
    for p in range(3):
        c0, w = BACK[p][1:]
        out_ref[:, c0:c0 + w] = (hidden_ref[:, c0:c0 + w] + result(0, p)).astype(BF16)
    for p in range(3):
        c0, w = BACK[p][1:]
        grad_ref[:, c0:c0 + w] = result(1, p) * gain_ref[:, c0:c0 + w]
    hidden = hidden_ref[...]
    scaled = grad_ref[...]
    scale = lax.rsqrt(jnp.mean(hidden * hidden, axis=1, keepdims=True) + EPSILON)
    along = jnp.mean(scaled * hidden, axis=1, keepdims=True)
    grad_ref[...] = cot_ref[...].astype(F32) + scale * scaled - hidden * (scale * scale * scale * along)
    for made in net.open:
        if id(made) not in done:
            made.wait_send()


def back(nexts, ranks, gin, fmids, wg, wu, wd, hidden, cot, gain, cid):
    vs = pl.BlockSpec(memory_space=pltpu.VMEM)
    anyspace = pl.BlockSpec(memory_space=pl.ANY)
    ws = [width for _, _, width in BACK]
    rows = [(4, 4, BLK, w) for w in ws]
    return pl.pallas_call(
        back_kernel,
        out_shape=(jax.ShapeDtypeStruct((128, D), BF16), jax.ShapeDtypeStruct((128, D), F32))
        + (jax.ShapeDtypeStruct((4, 4, BLK, FRONT[2][2] + FRONT[3][2]), BF16),)
        + tuple(jax.ShapeDtypeStruct(r, BF16) for r in rows) + tuple(jax.ShapeDtypeStruct((2,) + r, BF16) for r in rows) * 2,
        in_specs=[anyspace] * 3 + [vs] + [anyspace] * 6 + [vs] * 3, out_specs=(vs, vs) + (anyspace,) * 10,
        scratch_shapes=[vm(4, 2, 128, w) for w in ws] + [vm(*r) for r in rows] * 2
        + [vm(4, 4, BLK, 1024), vm(4, 4, BLK, 1, dtype=F32), vm(D, FF), vm(D, FF), vm(FF, D),
           vm(4, 4, BLK, FF, dtype=F32), vm(4, 4, BLK, FF, dtype=F32), vm(4, 4, BLK, FF), vm(4, 4, BLK, FF),
           vm(4, 4, BLK, max(ws)), vm(2, 4, BLK, D)]
        + [vm(4, 2, 128, w) for w in ws] + [vm(2, 4, 128, w) for w in ws] + [vm(2, 3, 128, w) for w in ws]
        + [pltpu.SemaphoreType.DMA((220,)), pltpu.SemaphoreType.DMA((220,)), pltpu.SemaphoreType.DMA((80,))],
        compiler_params=pltpu.CompilerParams(collective_id=cid, has_side_effects=True, vmem_limit_bytes=63 * 2**20),
    )(*nexts, ranks, gin, *fmids, wg, wu, wd, hidden, cot, gain)[:2]


def on_device(
    resid,
    query,
    keys,
    values,
    out_proj,
    norm_gain,
    expert_ids,
    route_gates,
    w_gate,
    w_up,
    w_down,
    cotangent,
):
    ids_t = expert_ids[0].T
    gates_t = route_gates[0].T
    gain = norm_gain[None]
    hidden, grad_arrived, mid2, mid3, next0, next1, next2, ranks = front(
        query[0], keys[0], values[0], out_proj, resid[0], gain, cotangent[0], ids_t, gates_t, 5)
    layer_out, grad_hidden = back(
        (next0, next1, next2), ranks, grad_arrived, (mid2, mid3), w_gate[0], w_up[0], w_down[0], hidden, cotangent[0], gain, 6)
    return (layer_out[None], grad_hidden[None])


def solution(mesh):
    placed = (
        P("ep", "cp", None),
        P("ep", "cp", None),
        P("ep", "cp", None),
        P("ep", "cp", None),
        P("cp", None),
        P(),
        P("ep", "cp", None),
        P("ep", "cp", None),
        P(("cp", "ep"), None, None),
        P(("cp", "ep"), None, None),
        P(("cp", "ep"), None, None),
        P("ep", "cp", None),
    )
    return jax.shard_map(
        on_device,
        mesh=mesh,
        in_specs=placed,
        out_specs=(P("ep", "cp", None), P("ep", "cp", None)),
        check_vma=False,
    )
```

```python
import functools
import jax
import jax.numpy as jnp
from jax import lax
from jax.experimental import pallas as pl
from jax.experimental.pallas import tpu as pltpu
from jax.sharding import PartitionSpec as P

MESH = pl.DeviceIdType.MESH
D = 2048
EPSILON = 1e-06
HEAD = 128
CAP = 10
BLK = 80
FF = 768
FRONT = ((0, 0, 512), (3, 512, 512), (0, 1024, 512), (3, 1536, 512))
BACK = ((0, 0, 640), (1, 640, 640), (2, 1280, 768))
ROLES = ((2, 0, 1), (0, 1, 2), (1, 2, 0), (2, 1, 0))
F32 = jnp.float32
BF16 = jnp.bfloat16


def coords():
    cp = lax.axis_index("cp")
    ep = lax.axis_index("ep")
    x = lax.div(ep, 8) * 2 + lax.rem(cp, 2)
    y = lax.rem(lax.div(ep, 2), 4)
    z = lax.div(cp, 2)
    return (x, y, z), lax.rem(ep, 2)


def place(pos, core):
    x, y, z = pos
    return (z * 2 + lax.rem(x, 2), lax.div(x, 2) * 8 + y * 2 + core)


def turn(v, d):
    return lax.rem(v + d, 4)


def moved(pos, axis, d):
    return tuple(turn(p, d) if i == axis else p for i, p in enumerate(pos))


class Net:
    def __init__(self, send, recv, local):
        self.pos, self.core = coords()
        self.send, self.recv, self.here = send, recv, local
        self.count = 0
        self.local_count = 0
        self.open = []

    def peer(self, axis, d):
        return place(moved(self.pos, axis, d), self.core)

    def mate(self):
        return place(self.pos, 1 - self.core)

    def copy(self, src, dst, target):
        n = self.count
        self.count += 1
        made = pltpu.make_async_remote_copy(
            src_ref=src, dst_ref=dst, send_sem=self.send.at[n], recv_sem=self.recv.at[n],
            device_id=target, device_id_type=MESH)
        self.open.append(made)
        return made

    def local(self, src, dst):
        n = self.local_count
        self.local_count += 1
        return pltpu.make_async_copy(src, dst, self.here.at[n])

    def greet(self, more=()):
        bar = pltpu.get_barrier_semaphore()
        self.targets = targets = list(more) + [self.peer(a, d) for a in range(3) for d in (1, 2, 3)] + [self.mate()]
        for t in targets:
            pl.semaphore_signal(bar, inc=1, device_id=t, device_id_type=MESH)

    def meet(self):
        pl.semaphore_wait(pltpu.get_barrier_semaphore(), len(self.targets))

    def finish(self):
        for made in self.open:
            made.wait_send()


def swap_matrix():
    r = lax.broadcasted_iota(jnp.int32, (320, 320), 0)
    c = lax.broadcasted_iota(jnp.int32, (320, 320), 1)
    b, rest = lax.div(r, 80), lax.rem(r, 80)
    a, w = lax.div(rest, 20), lax.rem(rest, 20)
    return (c == a * 80 + b * 20 + w).astype(F32).astype(BF16)


def ranks_to(ids_ref, gates_ref, out_ref, t):
    a1, a2, a3 = ROLES[t]
    q = lax.broadcasted_iota(jnp.int32, (128, 128), 0)
    digit = {a1: lax.div(q, 32), a2: lax.rem(lax.div(q, 4), 4), a3: lax.rem(q, 4)}
    core = lax.rem(lax.div(q, 16), 2)
    e0, e1 = place((digit[0], digit[1], digit[2]), core)
    expert = e0 * 16 + e1
    named = jnp.zeros((128, 128), F32)
    gate = jnp.zeros((128, 128), F32)
    for j in range(8):
        hit = ids_ref[j:j + 1, :] == expert
        named = named + jnp.where(hit, 1.0, 0.0)
        gate = gate + jnp.where(hit, gates_ref[j:j + 1, :], 0.0)
    lo = lax.broadcasted_iota(jnp.int32, (128, 128), 0)
    hi = lax.broadcasted_iota(jnp.int32, (128, 128), 1)
    upto = (lo <= hi).astype(F32).astype(BF16)
    seen = jnp.dot(named.astype(BF16), upto, preferred_element_type=F32)
    rank = jnp.where(named > 0.5, seen - 1.0, -1000.0)
    out_ref[:, :, 0] = rank.reshape(4, 2, 16, 128)
    out_ref[:, :, 1] = gate.reshape(4, 2, 16, 128)


def build_pick(ranks, core, pick_ref, gate_ref=None):
    rows = lax.broadcasted_iota(jnp.int32, (BLK, 128), 0).astype(F32)

    def step(e, carry):
        u, v = lax.div(e, 4), lax.rem(e, 4)
        total = jnp.zeros((BLK, 128), F32)
        for s in range(8):
            rank = ranks[s // 2, s % 2, core, 0, pl.ds(e, 1), :]
            hit = rank + float(CAP * s) == rows
            pick_ref[u, v, :, s * 128:(s + 1) * 128] = jnp.where(hit, 1.0, 0.0).astype(BF16)
            if gate_ref is not None:
                gate = ranks[s // 2, s % 2, core, 1, pl.ds(e, 1), :]
                total = total + jnp.where(hit, gate, 0.0)
        if gate_ref is not None:
            gate_ref[u, v] = jnp.sum(total, axis=1, keepdims=True)
        return carry
    lax.fori_loop(0, 16, step, 0)


class Ranks:
    def __init__(self, net, own_ranks, ranks):
        self.net, self.own_ranks, self.ranks = net, own_ranks, ranks
        self.sends, self.mates = [], []

    def prepare(self, ids_ref, gates_ref):
        for t in range(3):
            ranks_to(ids_ref, gates_ref, self.own_ranks.at[t], t)

    def send(self):
        net, pos, core = self.net, self.net.pos, self.net.core
        own_ranks, ranks = self.own_ranks, self.ranks
        for t in range(3):
            a1 = ROLES[t][0]
            cps = [net.copy(own_ranks.at[t, turn(pos[a1], d)], ranks.at[t, pos[a1], core], net.peer(a1, d)) for d in (1, 2, 3)]
            for cp in cps:
                cp.start()
            ranks[t, pos[a1], core] = own_ranks[t, pos[a1]]
            mate = net.copy(own_ranks.at[t, pos[a1], 1 - core], ranks.at[t, pos[a1], core, 1 - core], net.mate())
            mate.start()
            self.sends.append(cps)
            self.mates.append([mate])

    def forward(self):
        net, pos, core, ranks = self.net, self.net.pos, self.net.core, self.ranks
        for t in range(3):
            a1 = ROLES[t][0]
            for i, d in enumerate((1, 2, 3)):
                self.sends[t][i].wait_recv()
                a = turn(pos[a1], 4 - d)
                cp = net.copy(ranks.at[t, a, core, 1 - core], ranks.at[t, a, core, 1 - core], net.mate())
                cp.start()
                self.mates[t].append(cp)

    def wait(self, t):
        for cp in self.mates[t]:
            cp.wait_recv()


class Dispatch:
    def __init__(self, net, scaled, parts, ags, sels, mids, ends, ranks, pick, gate):
        self.net, self.scaled, self.parts = net, scaled, parts
        self.ags, self.sels, self.mids, self.ends = ags, sels, mids, ends
        self.ranks, self.pick, self.gate = ranks, pick, gate
        self.gathers, self.keeps, self.forwards, self.firsts, self.seconds = {}, {}, {}, {}, {}

    def gather(self, x_ref, which):
        net, pos, core = self.net, self.net.pos, self.net.core
        for p in which:
            t, c0, w = self.parts[p]
            a1 = ROLES[t][0]
            src = x_ref.at[:, c0:c0 + w]
            dst = self.ags[p].at[pos[a1], core]
            self.gathers[p] = [net.copy(src, dst, net.peer(a1, d)) for d in (1, 2, 3)]
            self.forwards[p] = [net.copy(src, dst, net.mate())]
            self.keeps[p] = [net.local(src, dst)]
            for cp in self.gathers[p] + self.forwards[p] + self.keeps[p]:
                cp.start()

    def forward(self, p):
        net, pos, core = self.net, self.net.pos, self.net.core
        a1 = ROLES[self.parts[p][0]][0]
        for i, d in enumerate((1, 2, 3)):
            self.gathers[p][i].wait_recv()
            at = self.ags[p].at[turn(pos[a1], 4 - d), core]
            cp = net.copy(at, at, net.mate())
            cp.start()
            self.forwards[p].append(cp)

    def gathered(self, p):
        for cp in self.forwards.get(p, ()):
            cp.wait_recv()
        for keep in self.keeps[p]:
            keep.wait()

    def build(self, p):
        build_pick(self.ranks.at[self.parts[p][0] % 3], self.net.core, self.pick, self.gate if self.scaled else None)

    def select(self, p):
        net, pos = self.net, self.net.pos
        t, c0, w = self.parts[p]
        a1, a2, a3 = ROLES[t]
        sel, mid, ag = self.sels[p], self.mids[p], self.ags[p]
        cps = [net.copy(sel.at[d - 1], mid.at[pos[a2]], net.peer(a2, d)) for d in (1, 2, 3)]
        for d in (1, 2, 3, 4):
            b = turn(pos[a2], d)
            mine = (lambda ref: ref[:, b]) if t == 3 else (lambda ref: ref[b])
            rows = jnp.dot(mine(self.pick).reshape(320, 1024), ag[...].reshape(1024, w), preferred_element_type=F32)
            if self.scaled:
                rows = rows * mine(self.gate).reshape(320, 1)
            sel[d - 1] = rows.astype(BF16).reshape(4, BLK, w)
            if d < 4:
                cps[d - 1].start()
        self.firsts[p] = cps

    def settle(self, p):
        keep = self.net.local(self.sels[p].at[3], self.mids[p].at[self.net.pos[ROLES[self.parts[p][0]][1]]])
        keep.start()
        for cp in self.firsts[p]:
            cp.wait_recv()
        keep.wait()

    def second(self, p):
        net, pos = self.net, self.net.pos
        t, c0, w = self.parts[p]
        a1, a2, a3 = ROLES[t]
        end = self.ends[p]
        sec, kept = [], []
        for i in range(4):
            a = turn(pos[a2], 4 - i)
            here = self.mids[p].at[a]
            if p in self.firsts:
                if i:
                    self.firsts[p][i - 1].wait_recv()
                else:
                    here = self.sels[p].at[3]
            at = end.at[(a, pos[a3]) if t == 3 else (pos[a3], a)]
            for d in (1, 2, 3):
                cp = net.copy(here.at[turn(pos[a3], d)], at, net.peer(a3, d))
                cp.start()
                sec.append(cp)
            keep = net.local(here.at[pos[a3]], at)
            keep.start()
            kept.append(keep)
        self.seconds[p] = sec, kept

    def arrived(self, p):
        sec, kept = self.seconds[p]
        for cp in sec:
            cp.wait_recv()
        for keep in kept:
            keep.wait()


def front_kernel(q_ref, k_ref, v_ref, w_ref, resid_ref, gain_ref, cot_ref, ids_ref, gates_ref,
                 hidden_ref, out_ref, mid2, mid3, next0, next1, next2, ranks_out, *scratch):
    (ag0, ag1, ag2, ag3, sel0, sel1, sel2, sel3, mid0, mid1, normed, own_ranks, pick, gate, qbuf, kbuf, vbuf, wbuf, att, part, rs, send, recv, here, local) = scratch
    net = Net(send, recv, here)
    pos, core = net.pos, net.core
    x, y, z = pos
    side = lax.rem(x, 2)
    other = x + 1 - 2 * side
    net.greet()
    ranks = Ranks(net, own_ranks, ranks_out)
    ranks.prepare(ids_ref, gates_ref)
    net.meet()
    ends = [out_ref.at[:, :, :, c0:c0 + w] for _, c0, w in FRONT[:2]] + [None, None]
    work = Dispatch(net, True, FRONT, (ag0, ag1, ag2, ag3), (sel0, sel1, sel2, sel3), (mid0, mid1, mid2, mid3), ends,
                    ranks_out, pick, gate)
    block = z * 2 + side

    def heads(ref, group, width):
        return ref.at[:, pl.ds(pl.multiple_of(group * width, width), width)]
    moves = []
    for d in (1, 2, 3):
        g = turn(z, d)
        moves.append(net.copy(heads(q_ref, g, 1024), qbuf.at[z], net.peer(2, d)))
    pairs = ((k_ref, kbuf), (v_ref, vbuf))
    kv = {d: [net.copy(heads(ref, turn(z, d), 128), buf.at[block], net.peer(2, d)) for ref, buf in pairs] for d in (1, 2, 3)}
    kv[0] = [net.copy(heads(ref, z, 128), buf.at[block], place((other, y, z), core)) for ref, buf in pairs]
    for d in (2, 1, 3, 0):
        for cp in kv[d]:
            cp.start()
    for cp in moves:
        cp.start()
    keeps = [pltpu.make_async_copy(heads(q_ref, z, 1024), qbuf.at[z], local.at[0]),
             pltpu.make_async_copy(heads(k_ref, z, 128), kbuf.at[block], local.at[1]),
             pltpu.make_async_copy(heads(v_ref, z, 128), vbuf.at[block], local.at[2]),
             pltpu.make_async_copy(w_ref, wbuf.at[side], local.at[3])]
    for cp in keeps:
        cp.start()
    ranks.send()
    work.gather(cot_ref, (0, 1))
    quarters = []
    for i, d in enumerate((1, 3)):
        at = pl.ds(pl.multiple_of((core * 2 + i) * 128, 128), 128)
        cp = net.copy(w_ref.at[at], wbuf.at[side, at], net.peer(0, d))
        cp.start()
        quarters.append(cp)
    for d in (1, 2, 3):
        for cp, (ref, buf) in zip(kv[d], pairs):
            cp.wait_recv()
            at = buf.at[turn(z, 4 - d) * 2 + side]
            on = net.copy(at, at, place((other, y, z), core))
            on.start()
            kv[0].append(on)
    ranks.forward()
    ranks.wait(0)
    work.build(0)
    for p in (0, 1):
        work.forward(p)
    work.gather(cot_ref, (2, 3))
    for p in (0, 1):
        work.gathered(p)
        work.select(p)
    ranks.wait(1)
    ranks.wait(2)
    for cp in quarters:
        cp.wait_recv()
    at = pl.ds(pl.multiple_of(core * 256, 256), 256)
    half = net.copy(wbuf.at[1 - side, at], wbuf.at[1 - side, at], net.mate())
    half.start()
    for cp in moves + kv[0]:
        cp.wait_recv()
    for cp in keeps:
        cp.wait()
    half.wait_recv()

    def attend(zp):
        span = 256 * (zp + 1)

        def pair(i, carry):
            lanes = pl.multiple_of(i * 256, 256)
            two = qbuf[zp, :, pl.ds(lanes, 256)]
            rows = jnp.concatenate([two[:, :128], two[:, 128:]], axis=0)
            scores = lax.dot_general(rows, kbuf[0:2 * zp + 2].reshape(span, 128), (((1,), (1,)), ((), ())),
                                     preferred_element_type=F32) * HEAD ** (-0.5)
            row = lax.broadcasted_iota(jnp.int32, (256, span), 0)
            col = lax.broadcasted_iota(jnp.int32, (256, span), 1)
            seen = col <= lax.rem(row, 128) + (2 * zp + side) * 128
            scores = jnp.where(seen, scores, -jnp.inf)
            weights = jnp.exp(scores - jnp.max(scores, axis=1, keepdims=True))
            probs = (weights / jnp.sum(weights, axis=1, keepdims=True)).astype(BF16)
            got = jnp.dot(probs, vbuf[0:2 * zp + 2].reshape(span, 128), preferred_element_type=F32).astype(BF16)
            att[zp, :, pl.ds(lanes, 256)] = jnp.concatenate([got[:128], got[128:]], axis=1)
            return carry
        lax.fori_loop(0, 4, pair, 0)

    def project(zp):
        def step(i, carry):
            lanes = pl.ds(pl.multiple_of(i * 512, 512), 512)
            total = jnp.dot(att[zp], wbuf[:, :, lanes].reshape(1024, 512), preferred_element_type=F32)
            part[zp, :, lanes] = total.astype(BF16)
            return carry
        lax.fori_loop(0, 4, step, 0)
    sends = {d: net.copy(part.at[turn(z, d)], rs.at[d - 1], net.peer(2, d)) for d in (2, 1, 3)}

    def turns(ds):
        def step(i, carry):
            far = ds[0] + i * (ds[1] - ds[0])
            zp = turn(z, far)
            for n in range(4):
                @pl.when(zp == n)
                def _():
                    attend(n)
            project(zp)
            for n, d in enumerate(ds):
                if d:
                    @pl.when(i == n)
                    def _():
                        sends[d].start()
            return carry
        lax.fori_loop(0, 2, step, 0)
    turns((2, 1))
    work.forward(2)
    work.forward(3)
    work.gathered(2)
    work.select(2)
    turns((3, 0))
    work.gathered(3)
    work.select(3)
    for p in range(2):
        work.second(p)
    total = resid_ref[...].astype(F32) + part[z].astype(F32)
    for d in (1, 2, 3):
        sends[d].wait_recv()
        total = total + rs[d - 1].astype(F32)
    hidden_ref[...] = total
    scale = lax.rsqrt(jnp.mean(total * total, axis=1, keepdims=True) + EPSILON)
    normed[...] = (total * scale * gain_ref[...]).astype(BF16)
    later = Dispatch(net, False, BACK, (next0, next1, next2), None, None, None, ranks_out, None, None)
    later.gather(normed, (0, 1, 2))
    for p in range(3):
        later.forward(p)
    for p in range(2):
        work.arrived(p)
    for p in (2, 3):
        work.settle(p)
    for p in range(3):
        later.gathered(p)
    net.finish()


def vm(*shape, dtype=BF16):
    return pltpu.VMEM(shape, dtype)


def front(q, k, v, w, resid, gain, cot, ids_t, gates_t, cid):
    vs = pl.BlockSpec(memory_space=pltpu.VMEM)
    anyspace = pl.BlockSpec(memory_space=pl.ANY)
    ws = [width for _, _, width in FRONT]
    half = ws[0] + ws[1]
    shapes = [(4, 4, BLK, half)] + [(4, 4, BLK, w) for w in ws[2:]] + [(4, 2, 128, w) for _, _, w in BACK]
    return pl.pallas_call(
        front_kernel,
        out_shape=(jax.ShapeDtypeStruct((128, D), F32),) + tuple(jax.ShapeDtypeStruct(r, BF16) for r in shapes)
        + (jax.ShapeDtypeStruct((3, 4, 2, 2, 2, 16, 128), F32),),
        in_specs=[anyspace] * 4 + [vs] * 5, out_specs=(vs,) + (anyspace,) * len(shapes) + (vs,),
        scratch_shapes=[vm(4, 2, 128, w) for w in ws] + [vm(4, 4, BLK, w) for w in ws] + [vm(4, 4, BLK, w) for w in ws[:2]]
        + [vm(128, D), vm(3, 4, 2, 2, 16, 128, dtype=F32), vm(4, 4, BLK, 1024), vm(4, 4, BLK, 1, dtype=F32),
           vm(4, 128, 1024), vm(8, 128, 128), vm(8, 128, 128), vm(2, 512, D), vm(4, 128, 1024), vm(4, 128, D), vm(3, 128, D),
           pltpu.SemaphoreType.DMA((180,)), pltpu.SemaphoreType.DMA((180,)), pltpu.SemaphoreType.DMA((30,)),
           pltpu.SemaphoreType.DMA((11,))],
        compiler_params=pltpu.CompilerParams(collective_id=cid, has_side_effects=True, vmem_limit_bytes=62 * 2**20),
    )(q, k, v, w, resid, gain, cot, ids_t, gates_t)


def back_kernel(next0, next1, next2, ranks, gin_ref, fmid2, fmid3, wg_ref, wu_ref, wd_ref, hidden_ref, cot_ref, gain_ref, out_ref, grad_ref, *scratch):
    (gin2, mid0, mid1, mid2, rmid0, rmid1, rmid2, new0, new1, new2,
     ag0, ag1, ag2, sel0, sel1, sel2, end0, end1, end2, pick, gate, wg, wu, wd, value, slope, inner, gup, stage, gin,
     part0, part1, part2, core0, core1, core2, rs0, rs1, rs2, send, recv, here) = scratch
    net = Net(send, recv, here)
    pos, core = net.pos, net.core
    ags, sels, ends = (ag0, ag1, ag2), (sel0, sel1, sel2), (end0, end1, end2)
    rmids, news, cores, rss = (rmid0, rmid1, rmid2), (new0, new1, new2), (core0, core1, core2), (rs0, rs1, rs2)
    loads = [net.local(a, b) for a, b in ((wg_ref, wg), (wu_ref, wu), (wd_ref, wd))]
    for cp in loads:
        cp.start()
    net.greet()
    work = Dispatch(net, False, BACK, ags, sels, (mid0, mid1, mid2), ends, ranks, pick, None)
    for p, ref in enumerate((next0, next1, next2)):
        work.keeps[p] = [net.local(ref, ags[p])]
        work.keeps[p][0].start()
    work.build(0)
    net.meet()
    for p in range(3):
        if p:
            work.build(p)
        work.gathered(p)
        work.select(p)
    for p in range(3):
        work.second(p)
    rest = Dispatch(net, True, FRONT[2:], None, None, (fmid2, fmid3),
                    [gin2.at[:, :, :, c:c + w] for c, w in ((0, FRONT[2][2]), (FRONT[2][2], FRONT[3][2]))], None, None, None)
    swap = swap_matrix()
    for cp in loads:
        cp.wait()

    def turned(rows):
        return jnp.dot(swap, rows, preferred_element_type=F32).astype(BF16)
    for p in range(3):
        t, c0, w = BACK[p]
        work.arrived(p)

        def pre(g, carry):
            rows = ends[p][g] if p != 1 else ends[p][:, g]
            rows = rows.reshape(320, w)
            if p:
                rows = turned(rows)
            for weight, total in ((wg, value), (wu, slope)):
                got = jnp.dot(rows, weight[c0:c0 + w, :], preferred_element_type=F32).reshape(4, BLK, FF)
                if p == 0:
                    total[g] = got
                elif p == 1:
                    total[g] += got
                else:
                    total[:, g] += got
            return carry
        lax.fori_loop(0, 4, pre, 0)

    def activate(i, carry):
        gate_pre, up_pre = value[i // 4, lax.rem(i, 4)], slope[i // 4, lax.rem(i, 4)]
        sigmoid = jax.nn.sigmoid(gate_pre)
        silu = gate_pre * sigmoid
        inner[i // 4, lax.rem(i, 4)] = (silu * up_pre).astype(BF16)
        value[i // 4, lax.rem(i, 4)] = silu
        slope[i // 4, lax.rem(i, 4)] = up_pre * (sigmoid * (1.0 + gate_pre * (1.0 - sigmoid)))
        return carry
    for p in range(2):
        rest.second(p)
    lax.fori_loop(0, 16, activate, 0)
    for cps in work.firsts.values():
        for cp in cps:
            cp.wait_send()
    for sec, _ in work.seconds.values():
        for i in range(3):
            sec[i].wait_send()
    done = set(id(cp) for cps in work.firsts.values() for cp in cps) | set(id(sec[i]) for sec, _ in work.seconds.values() for i in range(3))
    phase1, phase2, phase3, phase4 = {}, {}, {}, {}

    def first_back(k, p, rows_of, product):
        t, c0, w = BACK[p]
        a3 = ROLES[t][2]
        store = (sels, ends)[k][p]
        base = net.count
        cps = [net.copy(store.at[turn(pos[a3], d)], rmids[p].at[k, pos[a3]], net.peer(a3, d)) for d in (1, 2, 3)]

        def step(i, carry):
            g = turn(pos[a3], i + 1) if p != 1 else i
            got = product(rows_of(p, g), c0, w).astype(BF16).reshape(4, BLK, w)
            if p == 1:
                store[:, g] = got
            else:
                store[g] = got
                for d in (1, 2, 3):
                    @pl.when(i == d - 1)
                    def _():
                        cps[d - 1].start()
            return carry
        lax.fori_loop(0, 4, step, 0)
        if p == 1:
            for cp in cps:
                cp.start()
        phase1[k, p] = cps

    def inner_rows(ref):
        def rows(p, g):
            got = (ref[g] if p != 2 else ref[:, g]).reshape(320, FF)
            return turned(got) if p else got
        return rows
    for p in range(3):
        first_back(0, p, inner_rows(inner), lambda rows, c0, w: jnp.dot(rows, wd[:, c0:c0 + w], preferred_element_type=F32))
    nt = (((1,), (1,)), ((), ()))
    half = FRONT[2][1]
    fetch = [(net.local(gin_ref.at[g], gin.at[g % 2, :, :, :half]), net.local(gin2.at[g], gin.at[g % 2, :, :, half:])) for g in range(4)]
    for p in range(2):
        rest.arrived(p)
    for cp in fetch[0]:
        cp.start()
    for g in range(4):
        if g < 3:
            for cp in fetch[g + 1]:
                cp.start()
        for cp in fetch[g]:
            cp.wait()
        grad = lax.dot_general(gin[g % 2].reshape(320, D), wd[...], nt, preferred_element_type=F32).reshape(4, BLK, FF)
        inner[g] = (grad * slope[g]).astype(BF16)
        gup[g] = (grad * value[g]).astype(BF16)
    gate_rows, up_rows = inner_rows(inner), inner_rows(gup)

    def both(rows, c0, w):
        return (lax.dot_general(rows[0], wg[c0:c0 + w, :], nt, preferred_element_type=F32)
                + lax.dot_general(rows[1], wu[c0:c0 + w, :], nt, preferred_element_type=F32))
    for p in range(3):
        first_back(1, p, lambda p, g: (gate_rows(p, g), up_rows(p, g)), both)
    for k in range(2):
        for p in range(3):
            a1, a2, a3 = ROLES[BACK[p][0]]
            cps, kept = [], []
            for i in range(4):
                a = turn(pos[a3], 4 - i)
                if i:
                    phase1[k, p][i - 1].wait_recv()
                    at = rmids[p].at[k, a]
                else:
                    at = (sels, ends)[k][p].at[a]
                for d in (1, 2, 3):
                    cp = net.copy(at.at[turn(pos[a2], d)], news[p].at[k, pos[a2], a], net.peer(a2, d))
                    cp.start()
                    cps.append(cp)
                keep = net.local(at.at[pos[a2]], news[p].at[k, pos[a2], a])
                keep.start()
                kept.append(keep)
            phase2[k, p] = cps, kept
    parts = (ags, (part0, part1, part2))

    def pass_on(k, p):
        a1 = ROLES[BACK[p][0]][0]
        phase3[k, p].wait_recv()
        cores[p][k] = (cores[p][k].astype(F32) + parts[k][p][:, core].astype(F32)).astype(BF16)
        cps = [net.copy(cores[p].at[k, turn(pos[a1], d)], rss[p].at[k, d - 1], net.peer(a1, d)) for d in (1, 2, 3)]
        for cp in cps:
            cp.start()
        phase4[k, p] = cps
    order = [(k, p) for k in range(2) for p in range(3)]
    for n, (k, p) in enumerate(order):
        t, c0, w = BACK[p]
        build_pick(ranks.at[t], core, pick, gate)
        cps, kept = phase2[k, p]
        for cp in cps:
            cp.wait_recv()
        for keep in kept:
            keep.wait()
        load = net.local(news[p].at[k], stage.at[:, :, :, :w])
        load.start()
        load.wait()
        rows = stage[:, :, :, :w].reshape(1280, w)
        if k == 0:
            rows = (rows.astype(F32) * gate[...].reshape(1280, 1)).astype(BF16)
        total = lax.dot_general(pick[...].reshape(1280, 1024), rows, (((0,), (0,)), ((), ())), preferred_element_type=F32)
        parts[k][p][...] = total.astype(BF16).reshape(4, 2, 128, w)
        cp = net.copy(parts[k][p].at[:, 1 - core], cores[p].at[k], net.mate())
        cp.start()
        phase3[k, p] = cp
        if n:
            pass_on(*order[n - 1])
    pass_on(*order[-1])

    def result(k, p):
        a1 = ROLES[BACK[p][0]][0]
        total = cores[p][k, pos[a1]].astype(F32)
        for i, cp in enumerate(phase4[k, p]):
            cp.wait_recv()
            total = total + rss[p][k, i].astype(F32)
        return total
    for p in range(3):
        c0, w = BACK[p][1:]
        out_ref[:, c0:c0 + w] = (hidden_ref[:, c0:c0 + w] + result(0, p)).astype(BF16)
    for p in range(3):
        c0, w = BACK[p][1:]
        grad_ref[:, c0:c0 + w] = result(1, p) * gain_ref[:, c0:c0 + w]
    hidden = hidden_ref[...]
    scaled = grad_ref[...]
    scale = lax.rsqrt(jnp.mean(hidden * hidden, axis=1, keepdims=True) + EPSILON)
    along = jnp.mean(scaled * hidden, axis=1, keepdims=True)
    grad_ref[...] = cot_ref[...].astype(F32) + scale * scaled - hidden * (scale * scale * scale * along)
    for made in net.open:
        if id(made) not in done:
            made.wait_send()


def back(nexts, ranks, gin, fmids, wg, wu, wd, hidden, cot, gain, cid):
    vs = pl.BlockSpec(memory_space=pltpu.VMEM)
    anyspace = pl.BlockSpec(memory_space=pl.ANY)
    ws = [width for _, _, width in BACK]
    rows = [(4, 4, BLK, w) for w in ws]
    return pl.pallas_call(
        back_kernel,
        out_shape=(jax.ShapeDtypeStruct((128, D), BF16), jax.ShapeDtypeStruct((128, D), F32))
        + (jax.ShapeDtypeStruct((4, 4, BLK, FRONT[2][2] + FRONT[3][2]), BF16),)
        + tuple(jax.ShapeDtypeStruct(r, BF16) for r in rows) + tuple(jax.ShapeDtypeStruct((2,) + r, BF16) for r in rows) * 2,
        in_specs=[anyspace] * 3 + [vs] + [anyspace] * 6 + [vs] * 3, out_specs=(vs, vs) + (anyspace,) * 10,
        scratch_shapes=[vm(4, 2, 128, w) for w in ws] + [vm(*r) for r in rows] * 2
        + [vm(4, 4, BLK, 1024), vm(4, 4, BLK, 1, dtype=F32), vm(D, FF), vm(D, FF), vm(FF, D),
           vm(4, 4, BLK, FF, dtype=F32), vm(4, 4, BLK, FF, dtype=F32), vm(4, 4, BLK, FF), vm(4, 4, BLK, FF),
           vm(4, 4, BLK, max(ws)), vm(2, 4, BLK, D)]
        + [vm(4, 2, 128, w) for w in ws] + [vm(2, 4, 128, w) for w in ws] + [vm(2, 3, 128, w) for w in ws]
        + [pltpu.SemaphoreType.DMA((220,)), pltpu.SemaphoreType.DMA((220,)), pltpu.SemaphoreType.DMA((80,))],
        compiler_params=pltpu.CompilerParams(collective_id=cid, has_side_effects=True, vmem_limit_bytes=63 * 2**20),
    )(*nexts, ranks, gin, *fmids, wg, wu, wd, hidden, cot, gain)[:2]


def on_device(
    resid,
    query,
    keys,
    values,
    out_proj,
    norm_gain,
    expert_ids,
    route_gates,
    w_gate,
    w_up,
    w_down,
    cotangent,
):
    ids_t = expert_ids[0].T
    gates_t = route_gates[0].T
    gain = norm_gain[None]
    hidden, grad_arrived, mid2, mid3, next0, next1, next2, ranks = front(
        query[0], keys[0], values[0], out_proj, resid[0], gain, cotangent[0], ids_t, gates_t, 5)
    layer_out, grad_hidden = back(
        (next0, next1, next2), ranks, grad_arrived, (mid2, mid3), w_gate[0], w_up[0], w_down[0], hidden, cotangent[0], gain, 6)
    return (layer_out[None], grad_hidden[None])


def solution(mesh):
    placed = (
        P("ep", "cp", None),
        P("ep", "cp", None),
        P("ep", "cp", None),
        P("ep", "cp", None),
        P("cp", None),
        P(),
        P("ep", "cp", None),
        P("ep", "cp", None),
        P(("cp", "ep"), None, None),
        P(("cp", "ep"), None, None),
        P(("cp", "ep"), None, None),
        P("ep", "cp", None),
    )
    return jax.shard_map(
        on_device,
        mesh=mesh,
        in_specs=placed,
        out_specs=(P("ep", "cp", None), P("ep", "cp", None)),
        check_vma=False,
    )
```
